128 devices in a mesh: ctx: 32 (over x, y_hi, z), tp: 4 (over y_lo, core).
Axes of the slice: x: 4, y: 4 (y_hi: 2, y_lo: 2; y = y_hi * 2 + y_lo), z: 4, core: 2. Of those that a mesh axis runs over, the one named last changes fastest.
Arguments:
- tokens: bfloat16 [8192, 2048], P('ctx'), may hold values from -6 to 6
- query_weight: bfloat16 [2048, 2048], P(None, 'tp'), may hold values from -0.125 to 0.125
- key_weight: bfloat16 [2048, 2048], P(None, 'tp'), may hold values from -0.125 to 0.125
- value_weight: bfloat16 [2048, 2048], P(None, 'tp'), may hold values from -0.125 to 0.125
- output_weight: bfloat16 [2048, 2048], P('tp'), may hold values from -0.125 to 0.125
- gate_weight: bfloat16 [2048, 8192], P(None, 'tp'), may hold values from -0.125 to 0.125
- up_weight: bfloat16 [2048, 8192], P(None, 'tp'), may hold values from -0.125 to 0.125
- down_weight: bfloat16 [8192, 2048], P('tp'), may hold values from -0.0625 to 0.0625
- query_gain: float32 [2048], P('tp'), may hold values from 0.5 to 1.5
- key_gain: float32 [2048], P('tp'), may hold values from 0.5 to 1.5
- attention_gain: float32 [2048], replicated, may hold values from 0.5 to 1.5
- feedforward_gain: float32 [2048], replicated, may hold values from 0.5 to 1.5
- cotangent: bfloat16 [8192, 2048], P('ctx'), may hold values from -6 to 6
Outputs:
- layer_output: bfloat16 [8192, 2048], P('ctx')
- tokens_grad: float32 [8192, 2048], P('ctx')
- query_weight_grad: float32 [2048, 2048], P('ctx', 'tp')
- key_weight_grad: float32 [2048, 2048], P('ctx', 'tp')
- value_weight_grad: float32 [2048, 2048], P('ctx', 'tp')
- output_weight_grad: float32 [2048, 2048], P('tp', 'ctx')
- gate_weight_grad: float32 [2048, 8192], P('ctx', 'tp')
- up_weight_grad: float32 [2048, 8192], P('ctx', 'tp')
- down_weight_grad: float32 [8192, 2048], P('tp', 'ctx')
- query_gain_grad: float32 [2048], P('tp')
- key_gain_grad: float32 [2048], P('tp')
- attention_gain_grad: float32 [2048], replicated
- feedforward_gain_grad: float32 [2048], replicated
The draws below stay inside these ranges and needn't reach their ends.
All inputs are finite; a program needn't handle non-finite values.
Results may differ from the reference program's by a relative error of at most 0.035.
Values may be sent and summed in bfloat16 or wider, within the bound.
No kernel may reach another device: no remote copies, remote signals or barrier semaphores. Data moves between devices by JAX's collectives and lax.ppermute only.
A program may use at most 256 MiB of HBM per device.

```python
import math
import jax
import jax.numpy as jnp
from jax import lax

D = 2048
HEADS = 16
HD = 128
FF = 8192
LEN = 8192


def shard_levels(stream_key, dims, split, low, largest):
    level, own = 1.0, jax.random.fold_in(stream_key, 6)
    for dim, shards_of in split:
        draws = jnp.exp(jax.random.uniform(jax.random.fold_in(own, dim), (shards_of,), jnp.float32, low / len(split), largest / len(split)))
        level = level * jnp.repeat(draws, dims[dim] // shards_of).reshape([-1 if axis == dim else 1 for axis in range(len(dims))])
    return level


def bell_draw(rng, shape, spread, reach, pieces=(), kind=jnp.bfloat16):
    drawn = jax.random.normal(rng, shape, jnp.float32) * spread
    if len(pieces) > 0:
        drawn = shard_levels(rng, shape, pieces, -0.22, 0.18) * drawn
    return jnp.clip(drawn, min=-reach, max=reach).astype(kind)


def setup_inputs(seed: int = 0) -> dict:
    splits = jax.random.split(jax.random.key(seed), 14)
    tokens = bell_draw(splits[0], (LEN, D), 1.0, 6.0, ((0, 32),))
    query_weight = bell_draw(splits[1], (D, D), D ** -0.5, 0.125, ((1, 4),))
    key_weight = bell_draw(splits[2], (D, D), D ** -0.5, 0.125, ((1, 4),))
    value_weight = bell_draw(splits[3], (D, D), D ** -0.5, 0.125, ((1, 4),))
    output_weight = bell_draw(splits[4], (D, D), D ** -0.5, 0.125, ((0, 4),))
    gate_weight = bell_draw(splits[5], (D, FF), D ** -0.5, 0.125, ((1, 4),))
    up_weight = bell_draw(splits[6], (D, FF), D ** -0.5, 0.125, ((1, 4),))
    down_weight = bell_draw(splits[7], (FF, D), FF ** -0.5, 0.0625, ((0, 4),))
    query_gain = jnp.clip(1.0 + 0.1 * jax.random.normal(splits[8], (D,), jnp.float32), 0.5, 1.5)
    key_gain = jnp.clip(1.0 + 0.1 * jax.random.normal(splits[9], (D,), jnp.float32), 0.5, 1.5)
    attention_gain = jnp.clip(1.0 + 0.1 * jax.random.normal(splits[10], (D,), jnp.float32), 0.5, 1.5)
    feedforward_gain = jnp.clip(1.0 + 0.1 * jax.random.normal(splits[11], (D,), jnp.float32), 0.5, 1.5)
    cotangent = bell_draw(splits[12], (LEN, D), 1.0, 6.0, ((0, 32),))
    return {"tokens": tokens, "query_weight": query_weight, "key_weight": key_weight, "value_weight": value_weight, "output_weight": output_weight, "gate_weight": gate_weight, "up_weight": up_weight, "down_weight": down_weight, "query_gain": query_gain, "key_gain": key_gain, "attention_gain": attention_gain, "feedforward_gain": feedforward_gain, "cotangent": cotangent}


epsilon = 1e-06
rope_base = 500000.0
negative = -1e+30

@jax.custom_vjp
def low(v):
    return lax.optimization_barrier(v.astype(jnp.bfloat16)).astype(jnp.float32)

@jax.custom_vjp
def low_back(v):
    return v

def low_keep(v):
    return (low(v), None)

def low_pass(kept, grad):
    return (grad,)

def back_keep(v):
    return (v, None)

def back_low(kept, grad):
    return (low(grad),)
low.defvjp(low_keep, low_pass)
low_back.defvjp(back_keep, back_low)

def matmul(left, right):
    return jnp.dot(left, right, precision=lax.Precision.HIGHEST)

def row_scale(values_in):
    return lax.rsqrt(lax.optimization_barrier(jnp.mean(values_in * values_in, axis=-1, keepdims=True)) + epsilon)

def rope_tables(position_count):
    half_size = HD // 2
    frequency = 1.0 / rope_base ** (jnp.arange(half_size, dtype=jnp.float32) * 2.0 / HD)
    angles = jnp.arange(position_count, dtype=jnp.float32)[:, None] * frequency[None, :]
    return (jnp.cos(angles)[:, None, :], jnp.sin(angles)[:, None, :])

def rotate(values_in, cosine_table, sine_table):
    half_size = values_in.shape[-1] // 2
    lower_half = values_in[..., :half_size]
    upper_half = values_in[..., half_size:]
    return jnp.concatenate([lower_half * cosine_table - upper_half * sine_table, upper_half * cosine_table + lower_half * sine_table], axis=-1)

def attend(queries, keys, values):
    block_rows = math.gcd(512, LEN)
    block_count = LEN // block_rows
    score_scale = 1.0 / math.sqrt(HD)
    key_pos = jnp.arange(LEN)

    def one_block(block_in):
        query_block, offset = block_in
        scores = jnp.einsum('qhd,khd->hqk', query_block, keys, precision=lax.Precision.HIGHEST) * score_scale
        scores = low_back(scores)
        query_pos = offset + jnp.arange(block_rows)
        visible = key_pos[None, :] <= query_pos[:, None]
        masked = jnp.where(visible[None], scores, negative)
        row_max = lax.optimization_barrier(jnp.max(masked, axis=-1, keepdims=True))
        exps = jnp.exp(masked - row_max)
        probs_f = exps / lax.optimization_barrier(jnp.sum(exps, axis=-1, keepdims=True))
        return jnp.einsum('hqk,khd->qhd', low(probs_f), values, precision=lax.Precision.HIGHEST)
    blocks = queries.reshape(block_count, block_rows, HEADS, HD)
    offsets = jnp.arange(block_count) * block_rows
    return lax.map(jax.checkpoint(one_block), (blocks, offsets)).reshape(LEN, D)

def forward(tokens, query_weight, key_weight, value_weight, output_weight, gate_weight, up_weight, down_weight, query_gain, key_gain, attention_gain, feedforward_gain):
    query_raw = low_back(matmul(tokens, query_weight))
    key_raw = low_back(matmul(tokens, key_weight))
    value_low = low(low_back(matmul(tokens, value_weight)))
    cosine_table, sine_table = rope_tables(LEN)
    query_normed = query_raw * row_scale(query_raw) * query_gain
    key_normed = key_raw * row_scale(key_raw) * key_gain
    query_rot = low(rotate(query_normed.reshape(LEN, HEADS, HD), cosine_table, sine_table))
    key_rot = low(rotate(key_normed.reshape(LEN, HEADS, HD), cosine_table, sine_table))
    context = attend(query_rot, key_rot, value_low.reshape(LEN, HEADS, HD))
    context = low(low_back(context))
    attn_sum = low_back(matmul(context, output_weight))
    hidden = tokens + attn_sum * row_scale(attn_sum) * attention_gain
    hidden_low = low(hidden)
    gate_act = low_back(matmul(hidden_low, gate_weight))
    up_act = low_back(matmul(hidden_low, up_weight))
    mixed = low(jax.nn.silu(gate_act) * up_act)
    ffn_sum = low_back(matmul(mixed, down_weight))
    return hidden + ffn_sum * row_scale(ffn_sum) * feedforward_gain

def reference(tokens, query_weight, key_weight, value_weight, output_weight, gate_weight, up_weight, down_weight, query_gain, key_gain, attention_gain, feedforward_gain, cotangent):
    inputs = tuple((item.astype(jnp.float32) for item in (tokens, query_weight, key_weight, value_weight, output_weight, gate_weight, up_weight, down_weight, query_gain, key_gain, attention_gain, feedforward_gain)))
    result, pullback = jax.vjp(forward, *inputs)
    grads = pullback(cotangent.astype(jnp.float32))
    return (result.astype(jnp.bfloat16), grads[0], grads[1], grads[2], grads[3], grads[4], grads[5], grads[6], grads[7], grads[8], grads[9], grads[10], grads[11])
```

```python
import functools
import math

import jax
import jax.numpy as jnp
from jax import lax
from jax.experimental import pallas as pl
from jax.experimental.pallas import tpu as pltpu
from jax.sharding import Mesh
from jax.sharding import PartitionSpec as P

HD = 128
AXES = {"x": 4, "yh": 2, "z": 4, "yl": 2, "c": 2}
CTX = ("x", "yh", "z")
TP = ("yl", "c")
ROWS = 256
HALF = 128
HEADS = 4
EXTRA = 16
TILE = 1024

epsilon = 1e-06
rope_base = 500000.0
negative = -1e30
score_scale = 1.0 / math.sqrt(HD)


def product(left, right):
    return jnp.dot(left, right, preferred_element_type=jnp.float32)


def product_left(left, right):
    return lax.dot_general(
        left, right, (((0,), (0,)), ((), ())), preferred_element_type=jnp.float32
    )


def product_right(left, right):
    return lax.dot_general(
        left, right, (((1,), (1,)), ((), ())), preferred_element_type=jnp.float32
    )


def norm_back(values_in, scale_in, gain_in, grad_in):
    scaled_grad = grad_in * gain_in
    inner = jnp.mean(scaled_grad * values_in, axis=-1, keepdims=True)
    return scale_in * scaled_grad - values_in * scale_in**3 * inner


def exchange(values, axes):
    return lax.all_to_all(values, axes, split_axis=0, concat_axis=0, tiled=True)


def swap(values, axis):
    return lax.ppermute(values, axis, [(0, 1), (1, 0)])


def half_sum(part):
    theirs = swap(part[HALF:].astype(jnp.bfloat16), "c")
    mine = (part[:HALF] + theirs.astype(jnp.float32)).astype(jnp.bfloat16)
    far = swap(mine, "yl")
    return mine.astype(jnp.float32) + far.astype(jnp.float32)


def whole_rows(half):
    return jnp.concatenate([half, swap(half, "c")], axis=0)


def pass_x(values, step):
    return lax.ppermute(values, "x", [(i, (i + step) % 4) for i in range(4)])


def gather_x(half):
    near = jnp.concatenate([half] + [pass_x(half, step) for step in range(1, 4)], axis=0)
    return near, swap(near, "c")


def columns_x(x, *values):
    blocks = []
    for step in range(4):
        target = (x + step) % 4
        share = [
            lax.dynamic_slice_in_dim(v, target * (v.shape[1] // 4), v.shape[1] // 4, 1)
            for v in values
        ]
        share = share[0] if len(share) == 1 else jnp.concatenate(share, axis=1)
        blocks.append(pass_x(share, step) if step else share)
    return blocks


def weight_part(shared, blocks):
    near, far = shared
    total = product_left(near, jnp.concatenate([b[:HALF] for b in blocks], axis=0)) + product_left(
        far, jnp.concatenate([b[HALF:] for b in blocks], axis=0)
    )
    return total.astype(jnp.bfloat16)


def weight_sum(shared, blocks):
    part = weight_part(shared, blocks)
    rows, width = part.shape[0] // 32, part.shape[1]
    got = exchange(part.reshape(32, rows, width), CTX).reshape(4, 8, rows, width)
    return jnp.sum(got.astype(jnp.float32), axis=1)


def weight_scatter(shared, blocks):
    part = weight_part(shared, blocks)
    rows, width = part.shape[0] // 32, part.shape[1]
    part = jnp.swapaxes(part.reshape(4, 8, rows, width), 0, 1).reshape(32 * rows, width)
    return lax.psum_scatter(part, ("yh", "z"), scatter_dimension=0, tiled=True).reshape(
        4, rows, width
    )


def sum_pairs(values, names):
    for name in names:
        count = AXES[name]
        step = 1
        while step < count:
            values = values + lax.ppermute(values, name, [(i, i ^ step) for i in range(count)])
            step *= 2
    return values


def side_by_side(parts):
    return jnp.concatenate([parts[i] for i in range(parts.shape[0])], axis=1)


def turn_kernel(place_ref, q_ref, k_ref, v_ref, qs_ref, ks_ref, qg_ref, kg_ref, cos_ref, sin_ref, qo_ref, kvo_ref):
    def turned(values):
        return (values * cos_ref[...] + pltpu.roll(values, HD // 2, 1) * sin_ref[...]).astype(jnp.bfloat16)

    queries = turned(q_ref[...] * qs_ref[...] * qg_ref[...])
    keys = turned(k_ref[...] * ks_ref[...] * kg_ref[...])
    qo_ref[0] = queries
    for i in range(4):
        kvo_ref[0, i, 0] = keys
        kvo_ref[0, i, 1] = v_ref[...]


def turn(place, query_raw, key_raw, value_low, query_scale, key_scale, query_gain, key_gain, cosine, sine):
    block = pl.BlockSpec((ROWS, HD), lambda h, place: (0, h))
    column = pl.BlockSpec((ROWS, 1), lambda h, place: (0, 0))
    gain = pl.BlockSpec((1, HD), lambda h, place: (0, h))
    table = pl.BlockSpec((ROWS, HD), lambda h, place: (0, 0))
    return pl.pallas_call(
        turn_kernel,
        grid_spec=pltpu.PrefetchScalarGridSpec(
            num_scalar_prefetch=1,
            grid=(HEADS,),
            in_specs=[block, block, block, column, column, gain, gain, table, table],
            out_specs=[
                pl.BlockSpec((1, ROWS, HD), lambda h, place: ((h - place[0]) & 3, 0, 0)),
                pl.BlockSpec((1, 4, 2, ROWS, HD), lambda h, place: (h, 0, 0, 0, 0)),
            ],
        ),
        out_shape=[
            jax.ShapeDtypeStruct((4, ROWS, HD), jnp.bfloat16),
            jax.ShapeDtypeStruct((4, 4, 2, ROWS, HD), jnp.bfloat16),
        ],
        name="turn",
    )(place, query_raw, key_raw, value_low, query_scale, key_scale, query_gain, key_gain, cosine, sine)


def to_rows(values):
    rows = []
    for _ in range(3):
        high = values.astype(jnp.bfloat16).astype(jnp.float32)
        rows += [high[:, :HD], high[:, HD:]]
        values = values - high
    return rows


def row_block(rows):
    rows = rows + [jnp.zeros((1, HD), jnp.float32)] * (EXTRA - len(rows))
    return jnp.concatenate(rows, axis=0).astype(jnp.bfloat16)


def from_rows(block, at):
    block = block.astype(jnp.float32)
    sides = [
        block[at + i : at + i + 1] + block[at + i + 2 : at + i + 3] + block[at + i + 4 : at + i + 5]
        for i in range(2)
    ]
    return jnp.concatenate(sides, axis=1)


def where_block(b, place):
    return ((place[0] - (b & 3)) & 3) * 2 + (place[1] ^ (b >> 2))


def keep(place_ref):
    zone, core = place_ref[2], place_ref[3]
    key_row = lax.broadcasted_iota(jnp.int32, (TILE, ROWS), 0)
    query_row = lax.broadcasted_iota(jnp.int32, (TILE, ROWS), 1)
    flip = core * HALF
    key_pos = (key_row & ~(ROWS - 1)) | ((key_row & (ROWS - 1)) ^ flip)
    query_pos = zone * ROWS + (query_row ^ flip)
    return key_pos <= query_pos


def attend_kernel(place_ref, q_ref, kv_ref, out_ref, turned_ref, max_ref, total_ref, sum_ref):
    block = pl.program_id(0)
    column, side = (place_ref[0] - (block & 3)) & 3, place_ref[1] ^ (block >> 2)
    own_side = place_ref[1]

    @pl.when(block == 0)
    def _():
        for i in range(4):
            for j in range(4):
                turned_ref[i, :, j * ROWS : (j + 1) * ROWS] = jnp.transpose(kv_ref[i, j, 1])

    max_ref[...] = jnp.full_like(max_ref, negative)
    total_ref[...] = jnp.zeros_like(total_ref)
    sum_ref[...] = jnp.zeros_like(sum_ref)
    queries = q_ref[0]

    def tile(i, masked):
        keys = kv_ref[i, :, 0].reshape(TILE, HD)
        scores = product_right(keys, queries) * score_scale
        if masked:
            scores = jnp.where(keep(place_ref), scores, negative)
        old_max = max_ref[...]
        new_max = jnp.maximum(old_max, jnp.max(scores, axis=0, keepdims=True))
        weights = jnp.exp(scores - new_max)
        fade = jnp.exp(old_max - new_max)
        max_ref[...] = new_max
        total_ref[...] = total_ref[...] * fade + jnp.sum(weights, axis=0, keepdims=True)
        sum_ref[...] = sum_ref[...] * fade + product(turned_ref[i], weights.astype(jnp.bfloat16))

    @pl.loop(0, column + jnp.where(side > own_side, 1, 0))
    def _(i):
        tile(i, False)

    @pl.when(side == own_side)
    def _():
        tile(column, True)

    seen = total_ref[...] > 0.0
    safe = jnp.where(seen, total_ref[...], 1.0)
    out_ref[0, :ROWS] = jnp.transpose(sum_ref[...] / safe).astype(jnp.bfloat16)
    lse = jnp.where(seen, max_ref[...] + jnp.log(safe), negative)
    out_ref[0, ROWS:] = row_block(to_rows(lse))


def attend(place, queries, keys_values):
    return pl.pallas_call(
        attend_kernel,
        grid_spec=pltpu.PrefetchScalarGridSpec(
            num_scalar_prefetch=1,
            grid=(8,),
            in_specs=[
                pl.BlockSpec((1, ROWS, HD), lambda b, place: (b, 0, 0)),
                pl.BlockSpec((4, 4, 2, ROWS, HD), lambda b, place: (0, 0, 0, 0, 0)),
            ],
            out_specs=pl.BlockSpec(
                (1, ROWS + EXTRA, HD), lambda b, place: (where_block(b, place), 0, 0)
            ),
            scratch_shapes=[
                pltpu.VMEM((4, HD, TILE), jnp.bfloat16),
                pltpu.VMEM((1, ROWS), jnp.float32),
                pltpu.VMEM((1, ROWS), jnp.float32),
                pltpu.VMEM((HD, ROWS), jnp.float32),
            ],
        ),
        out_shape=jax.ShapeDtypeStruct((8, ROWS + EXTRA, HD), jnp.bfloat16),
        compiler_params=pltpu.CompilerParams(vmem_limit_bytes=40 * 2**20),
        name="attend",
    )(place, queries, keys_values)


def merge_kernel(part_ref, context_ref, low_ref, log_ref):
    lse = jnp.concatenate([from_rows(part_ref[0, i, ROWS:], 0) for i in range(2)], axis=0)
    most = jnp.max(lse, axis=0, keepdims=True)
    shares = jnp.exp(lse - most)
    total = jnp.sum(shares, axis=0, keepdims=True)
    shares = shares / total
    context = jnp.zeros((ROWS, HD), jnp.float32)
    for i in range(2):
        share = jnp.transpose(jnp.broadcast_to(shares[i : i + 1], (HD, ROWS)))
        context = context + share * part_ref[0, i, :ROWS].astype(jnp.float32)
    context_ref[...] = context
    low_ref[...] = context.astype(jnp.bfloat16)
    log_ref[0] = most + jnp.log(total)


def merge(parts):
    block = pl.BlockSpec((ROWS, HD), lambda h: (0, h))
    return pl.pallas_call(
        merge_kernel,
        grid=(HEADS,),
        in_specs=[pl.BlockSpec((1, 2, ROWS + EXTRA, HD), lambda h: (h, 0, 0, 0))],
        out_specs=[block, block, pl.BlockSpec((1, 1, ROWS), lambda h: (h, 0, 0))],
        out_shape=[
            jax.ShapeDtypeStruct((ROWS, HEADS * HD), jnp.float32),
            jax.ShapeDtypeStruct((ROWS, HEADS * HD), jnp.bfloat16),
            jax.ShapeDtypeStruct((HEADS, 1, ROWS), jnp.float32),
        ],
        name="merge",
    )(parts)


def spread_kernel(grad_ref, context_ref, log_ref, out_ref):
    grad = grad_ref[...]
    dots = jnp.transpose(grad.astype(jnp.float32) * context_ref[...])
    row_dot = jnp.sum(dots, axis=0, keepdims=True)
    rows = row_block(to_rows(log_ref[0]) + to_rows(row_dot))
    for i in range(2):
        out_ref[0, i, :ROWS] = grad
        out_ref[0, i, ROWS:] = rows


def spread(context_grad, context, log_total):
    block = pl.BlockSpec((ROWS, HD), lambda h: (0, h))
    return pl.pallas_call(
        spread_kernel,
        grid=(HEADS,),
        in_specs=[block, block, pl.BlockSpec((1, 1, ROWS), lambda h: (h, 0, 0))],
        out_specs=pl.BlockSpec((1, 2, ROWS + EXTRA, HD), lambda h: (h, 0, 0, 0)),
        out_shape=jax.ShapeDtypeStruct((4, 2, ROWS + EXTRA, HD), jnp.bfloat16),
        name="spread",
    )(context_grad, context, log_total)


def attend_back_kernel(
    place_ref, q_ref, grad_ref, kv_ref, dq_ref, dkv_ref, turned_ref, total_ref, query_ref
):
    block = pl.program_id(0)
    column, side = (place_ref[0] - (block & 3)) & 3, place_ref[1] ^ (block >> 2)
    own_side = place_ref[1]

    @pl.when(block == 0)
    def _():
        total_ref[...] = jnp.zeros_like(total_ref)
        for i in range(4):
            for j in range(4):
                turned_ref[i, :, j * ROWS : (j + 1) * ROWS] = jnp.transpose(kv_ref[i, j, 0])

    query_ref[...] = jnp.zeros_like(query_ref)
    queries = q_ref[0]
    grads = grad_ref[0, :ROWS]
    log_total = from_rows(grad_ref[0, ROWS:], 0)
    row_dot = from_rows(grad_ref[0, ROWS:], 6)

    def tile(i, masked):
        keys = kv_ref[i, :, 0].reshape(TILE, HD)
        values = kv_ref[i, :, 1].reshape(TILE, HD)
        scores = product_right(keys, queries) * score_scale - log_total
        if masked:
            scores = jnp.where(keep(place_ref), scores, negative)
        weights = jnp.exp(scores)
        weight_grad = product_right(values, grads)
        score_grad = (weights * (weight_grad - row_dot)).astype(jnp.bfloat16)
        total_ref[i, 1] += product(weights.astype(jnp.bfloat16), grads)
        total_ref[i, 0] += product(score_grad, queries)
        query_ref[...] += product(turned_ref[i], score_grad)

    @pl.loop(0, column + jnp.where(side > own_side, 1, 0))
    def _(i):
        tile(i, False)

    @pl.when(side == own_side)
    def _():
        tile(column, True)

    dq_ref[0] = jnp.transpose(query_ref[...] * score_scale).astype(jnp.bfloat16)

    @pl.when(block == 7)
    def _():
        for i in range(4):
            for j in range(4):
                rows = slice(j * ROWS, (j + 1) * ROWS)
                dkv_ref[i, j, 0] = (total_ref[i, 0, rows] * score_scale).astype(jnp.bfloat16)
                dkv_ref[i, j, 1] = total_ref[i, 1, rows].astype(jnp.bfloat16)


def attend_back(place, queries, grads, keys_values):
    whole = pl.BlockSpec((4, 4, 2, ROWS, HD), lambda b, place: (0, 0, 0, 0, 0))
    block = pl.BlockSpec((1, ROWS, HD), lambda b, place: (b, 0, 0))
    return pl.pallas_call(
        attend_back_kernel,
        grid_spec=pltpu.PrefetchScalarGridSpec(
            num_scalar_prefetch=1,
            grid=(8,),
            in_specs=[
                block,
                pl.BlockSpec(
                    (1, ROWS + EXTRA, HD), lambda b, place: (where_block(b, place), 0, 0)
                ),
                whole,
            ],
            out_specs=[block, whole],
            scratch_shapes=[
                pltpu.VMEM((4, HD, TILE), jnp.bfloat16),
                pltpu.VMEM((4, 2, TILE, HD), jnp.float32),
                pltpu.VMEM((HD, ROWS), jnp.float32),
            ],
        ),
        out_shape=[
            jax.ShapeDtypeStruct((8, ROWS, HD), jnp.bfloat16),
            jax.ShapeDtypeStruct((4, 4, 2, ROWS, HD), jnp.bfloat16),
        ],
        compiler_params=pltpu.CompilerParams(vmem_limit_bytes=48 * 2**20),
        name="attend_back",
    )(place, queries, grads, keys_values)


def turn_back_kernel(
    place_ref, dq_ref, dkv_ref, q_ref, k_ref, qg_ref, kg_ref, cos_ref, sin_ref, qo_ref, ko_ref, vo_ref, qi_ref, ki_ref
):
    def turned(values):
        return values * cos_ref[...] - pltpu.roll(values, HD // 2, 1) * sin_ref[...]

    head = pl.program_id(0)
    queries = dq_ref[0].astype(jnp.float32)
    keys = jnp.zeros((ROWS, HD), jnp.float32)
    values = jnp.zeros((ROWS, HD), jnp.float32)
    for i in range(4):
        keys = keys + dkv_ref[0, i, 0].astype(jnp.float32)
        values = values + dkv_ref[0, i, 1].astype(jnp.float32)
    queries, keys = turned(queries), turned(keys)
    qo_ref[...] = queries
    ko_ref[...] = keys
    vo_ref[...] = values.astype(jnp.bfloat16)

    @pl.when(head == 0)
    def _():
        qi_ref[...] = jnp.zeros_like(qi_ref)
        ki_ref[...] = jnp.zeros_like(ki_ref)

    qi_ref[...] += queries * qg_ref[...] * q_ref[...]
    ki_ref[...] += keys * kg_ref[...] * k_ref[...]


def turn_back(place, query_grad, key_value_grad, query_raw, key_raw, query_gain, key_gain, cosine, sine):
    block = pl.BlockSpec((ROWS, HD), lambda h, place: (0, h))
    gain = pl.BlockSpec((1, HD), lambda h, place: (0, h))
    table = pl.BlockSpec((ROWS, HD), lambda h, place: (0, 0))
    wide = (ROWS, HEADS * HD)
    return pl.pallas_call(
        turn_back_kernel,
        grid_spec=pltpu.PrefetchScalarGridSpec(
            num_scalar_prefetch=1,
            grid=(HEADS,),
            in_specs=[
                pl.BlockSpec((1, ROWS, HD), lambda h, place: ((h - place[0]) & 3, 0, 0)),
                pl.BlockSpec((1, 4, 2, ROWS, HD), lambda h, place: (h, 0, 0, 0, 0)),
                block,
                block,
                gain,
                gain,
                table,
                table,
            ],
            out_specs=[block, block, block, table, table],
        ),
        out_shape=[
            jax.ShapeDtypeStruct(wide, jnp.float32),
            jax.ShapeDtypeStruct(wide, jnp.float32),
            jax.ShapeDtypeStruct(wide, jnp.bfloat16),
            jax.ShapeDtypeStruct((ROWS, HD), jnp.float32),
            jax.ShapeDtypeStruct((ROWS, HD), jnp.float32),
        ],
        name="turn_back",
    )(place, query_grad, key_value_grad, query_raw, key_raw, query_gain, key_gain, cosine, sine)


def per_device(
    tokens,
    query_weight,
    key_weight,
    value_weight,
    output_weight,
    gate_weight,
    up_weight,
    down_weight,
    query_gain,
    key_gain,
    attention_gain,
    feedforward_gain,
    cotangent,
):
    full_width = tokens.shape[1]
    x, yh, z, core = (lax.axis_index(name) for name in ("x", "yh", "z", "c"))
    place = jnp.stack([x, yh, z, core]).astype(jnp.int32)

    def own_first(values):
        return jnp.where(core == 0, values, jnp.concatenate([values[HALF:], values[:HALF]], axis=0))

    def sum_rows(first, second):
        both = jnp.stack([own_first(first), own_first(second)])
        both = lax.psum(both, TP)
        return jnp.stack([own_first(both[0]), own_first(both[1])])

    def own_rows(values):
        return lax.dynamic_slice_in_dim(values, core * HALF, HALF, 0)

    def natural_rows(mine):
        theirs = swap(mine, "c")
        return jnp.where(
            core == 0,
            jnp.concatenate([mine, theirs], axis=0),
            jnp.concatenate([theirs, mine], axis=0),
        )

    positions = (8 * x + 4 * yh + z) * ROWS + (jnp.arange(ROWS, dtype=jnp.int32) ^ (core * HALF))
    half_size = HD // 2
    frequency = 1.0 / rope_base ** (jnp.arange(half_size, dtype=jnp.float32) * 2.0 / HD)
    angles = positions.astype(jnp.float32)[:, None] * frequency[None, :]
    cosine, sine = jnp.cos(angles), jnp.sin(angles)
    cosine_table = jnp.concatenate([cosine, cosine], axis=1)
    sine_table = jnp.concatenate([-sine, sine], axis=1)
    query_row_gain, key_row_gain = query_gain[None], key_gain[None]

    tokens_own = own_rows(tokens)
    tokens_first = own_first(tokens)
    query_raw = product(tokens_first, query_weight)
    key_raw = product(tokens_first, key_weight)
    value_low = product(tokens_first, value_weight).astype(jnp.bfloat16)
    squares = sum_rows(jnp.sum(query_raw * query_raw, axis=1), jnp.sum(key_raw * key_raw, axis=1))
    scales = lax.rsqrt(squares / full_width + epsilon)
    query_scale, key_scale = scales[0][:, None], scales[1][:, None]
    query_sent, key_value_sent = turn(
        place,
        query_raw,
        key_raw,
        value_low,
        query_scale,
        key_scale,
        query_row_gain,
        key_row_gain,
        cosine_table,
        sine_table,
    )
    queries = jnp.stack(
        [query_sent[0]] + [pass_x(query_sent[step], step) for step in range(1, 4)]
    )
    queries = jnp.concatenate([queries, swap(queries, "yh")], axis=0)
    keys_values = exchange(key_value_sent.reshape(16, 2, ROWS, HD), ("x", "z")).reshape(
        4, 4, 2, ROWS, HD
    )
    tokens_all = gather_x(tokens_own)
    part = exchange(attend(place, queries, keys_values), ("x", "yh"))
    context, context_low, log_total = merge(part.reshape(4, 2, ROWS + EXTRA, HD))
    context_columns = columns_x(x, context_low)

    attn_sum = half_sum(product(context_low, output_weight))
    attn_scale = lax.rsqrt(jnp.mean(attn_sum * attn_sum, axis=-1, keepdims=True) + epsilon)
    hidden = tokens_own.astype(jnp.float32) + attn_sum * attn_scale * attention_gain
    hidden_own = hidden.astype(jnp.bfloat16)
    hidden_low = whole_rows(hidden_own)
    hidden_all = gather_x(hidden_own)
    gate_act = product(hidden_low, gate_weight)
    up_act = product(hidden_low, up_weight)
    gate_sigmoid = jax.nn.sigmoid(gate_act)
    gate_silu = gate_act * gate_sigmoid
    mixed_low = (gate_silu * up_act).astype(jnp.bfloat16)
    mixed_columns = columns_x(x, mixed_low)

    ffn_sum = half_sum(product(mixed_low, down_weight))
    ffn_scale = lax.rsqrt(jnp.mean(ffn_sum * ffn_sum, axis=-1, keepdims=True) + epsilon)
    layer_output = natural_rows(
        (hidden + ffn_sum * ffn_scale * feedforward_gain).astype(jnp.bfloat16)
    )
    upstream = own_rows(cotangent).astype(jnp.float32)
    ffn_gain_term = jnp.sum(upstream * ffn_sum * ffn_scale, axis=0)
    ffn_grad_own = norm_back(ffn_sum, ffn_scale, feedforward_gain, upstream).astype(jnp.bfloat16)
    ffn_grad = whole_rows(ffn_grad_own)
    ffn_grad_all = gather_x(ffn_grad_own)
    mixed_grad = product_right(ffn_grad, down_weight)
    gate_grad = (
        mixed_grad * up_act * gate_sigmoid * (1.0 + gate_act * (1.0 - gate_sigmoid))
    ).astype(jnp.bfloat16)
    up_grad = (mixed_grad * gate_silu).astype(jnp.bfloat16)
    gate_up_columns = columns_x(x, gate_grad, up_grad)
    hidden_part = product_right(gate_grad, gate_weight) + product_right(up_grad, up_weight)
    hidden_grad = upstream + half_sum(hidden_part)
    attn_gain_term = jnp.sum(hidden_grad * attn_sum * attn_scale, axis=0)
    attn_grad_own = norm_back(attn_sum, attn_scale, attention_gain, hidden_grad).astype(
        jnp.bfloat16
    )
    attn_grad = whole_rows(attn_grad_own)
    attn_grad_all = gather_x(attn_grad_own)
    context_grad = product_right(attn_grad, output_weight).astype(jnp.bfloat16)
    grads = exchange(
        spread(context_grad, context, log_total).reshape(8, ROWS + EXTRA, HD), ("x", "yh")
    )

    down_weight_part = weight_scatter(ffn_grad_all, mixed_columns)
    gate_up_weight_part = weight_scatter(hidden_all, gate_up_columns)
    output_weight_part = weight_scatter(attn_grad_all, context_columns)

    query_back, key_value_back = attend_back(place, queries, grads, keys_values)
    query_back = (
        query_back[:4].astype(jnp.float32) + swap(query_back[4:], "yh").astype(jnp.float32)
    ).astype(jnp.bfloat16)
    query_back = jnp.stack(
        [query_back[0]] + [pass_x(query_back[step], -step) for step in range(1, 4)]
    )
    key_value_back = exchange(key_value_back.reshape(16, 2, ROWS, HD), ("x", "z")).reshape(
        4, 4, 2, ROWS, HD
    )
    query_normed_grad, key_normed_grad, value_grad, query_inner, key_inner = turn_back(
        place,
        query_back,
        key_value_back,
        query_raw,
        key_raw,
        query_row_gain,
        key_row_gain,
        cosine_table,
        sine_table,
    )
    inner = sum_rows(jnp.sum(query_inner, axis=1), jnp.sum(key_inner, axis=1)) / full_width
    query_raw_grad = (
        query_scale * query_gain * query_normed_grad
        - query_raw * query_scale**3 * inner[0][:, None]
    ).astype(jnp.bfloat16)
    key_raw_grad = (
        key_scale * key_gain * key_normed_grad - key_raw * key_scale**3 * inner[1][:, None]
    ).astype(jnp.bfloat16)
    low_columns = columns_x(x, query_raw_grad, key_raw_grad, value_grad)
    tokens_part = (
        product_right(query_raw_grad, query_weight)
        + product_right(key_raw_grad, key_weight)
        + product_right(value_grad, value_weight)
    )
    tokens_grad = natural_rows(hidden_grad + half_sum(tokens_part))
    low_weight_grad = weight_sum(tokens_all, low_columns)
    late_weight_grad = exchange(
        jnp.concatenate([gate_up_weight_part, down_weight_part, output_weight_part], axis=2), "x"
    ).astype(jnp.float32)

    gains = sum_pairs(
        jnp.concatenate(
            [
                jnp.sum(query_normed_grad * query_raw * query_scale, axis=0),
                jnp.sum(key_normed_grad * key_raw * key_scale, axis=0),
                sum_pairs(jnp.concatenate([attn_gain_term, ffn_gain_term]), ("c",)),
            ]
        ),
        CTX,
    )
    return (
        layer_output,
        tokens_grad,
        side_by_side(low_weight_grad[:, :, 0:128]),
        side_by_side(low_weight_grad[:, :, 128:256]),
        side_by_side(low_weight_grad[:, :, 256:384]),
        jnp.transpose(side_by_side(late_weight_grad[:, :, 1536:1664])),
        side_by_side(late_weight_grad[:, :, 0:512]),
        side_by_side(late_weight_grad[:, :, 512:1024]),
        jnp.transpose(side_by_side(late_weight_grad[:, :, 1024:1536])),
        gains[0:512],
        gains[512:1024],
        gains[1024:3072],
        gains[3072:5120],
    )


def solution(mesh):
    chips = Mesh(mesh.devices.reshape(tuple(AXES.values())), tuple(AXES))
    in_specs = (
        P(CTX, None),
        P(None, TP),
        P(None, TP),
        P(None, TP),
        P(TP, None),
        P(None, TP),
        P(None, TP),
        P(TP, None),
        P(TP),
        P(TP),
        P(),
        P(),
        P(CTX, None),
    )
    out_specs = (
        P(CTX, None),
        P(CTX, None),
        P(CTX, TP),
        P(CTX, TP),
        P(CTX, TP),
        P(TP, CTX),
        P(CTX, TP),
        P(CTX, TP),
        P(TP, CTX),
        P(TP),
        P(TP),
        P(),
        P(),
    )
    return jax.shard_map(
        per_device, mesh=chips, in_specs=in_specs, out_specs=out_specs, check_vma=False
    )
```

```python
import functools
import math

import jax
import jax.numpy as jnp
from jax import lax
from jax.experimental import pallas as pl
from jax.experimental.pallas import tpu as pltpu
from jax.sharding import Mesh
from jax.sharding import PartitionSpec as P

HD = 128
AXES = {"x": 4, "yh": 2, "z": 4, "yl": 2, "c": 2}
CTX = ("x", "yh", "z")
TP = ("yl", "c")
ROWS = 256
HALF = 128
HEADS = 4
EXTRA = 16
LIMIT = 60 * 2**20
GAIN_ROWS = 8
STEP = 512
GAINS = 32
TILE = 1024

epsilon = 1e-06
rope_base = 500000.0
negative = -1e30
score_scale = 1.0 / math.sqrt(HD)
log2e = math.log2(math.e)


def product(left, right):
    return jnp.dot(left, right, preferred_element_type=jnp.float32)


def product_left(left, right):
    return lax.dot_general(
        left, right, (((0,), (0,)), ((), ())), preferred_element_type=jnp.float32
    )


def product_right(left, right):
    return lax.dot_general(
        left, right, (((1,), (1,)), ((), ())), preferred_element_type=jnp.float32
    )


def norm_back(values_in, scale_in, gain_in, grad_in):
    scaled_grad = grad_in * gain_in
    inner = jnp.mean(scaled_grad * values_in, axis=-1, keepdims=True)
    return scale_in * scaled_grad - values_in * scale_in**3 * inner


def exchange(values, axes):
    return lax.all_to_all(values, axes, split_axis=0, concat_axis=0, tiled=True)


def swap(values, axis):
    return lax.ppermute(values, axis, [(0, 1), (1, 0)])


def half_sum(part):
    theirs = swap(part[HALF:].astype(jnp.bfloat16), "c")
    mine = (part[:HALF] + theirs.astype(jnp.float32)).astype(jnp.bfloat16)
    far = swap(mine, "yl")
    return mine.astype(jnp.float32) + far.astype(jnp.float32)


def together(*values):
    return lax.optimization_barrier(values)


def send(values, axis, step):
    return lax.ppermute(values, axis, [(i, (i + step) % 4) for i in range(4)])


def gather(half, axis):
    return lax.all_gather(half, axis, axis=0, tiled=True).reshape(-1, half.shape[0], HALF)


def pack_kernel(place_ref, in_ref, out_ref):
    for i in range(16):
        out_ref[i] = in_ref[:, head_columns(i)]


def pack(place, values):
    return call(pack_kernel, "pack", [((16, ROWS, HD), jnp.bfloat16)], place, values)


def with_other_core(near):
    return near, swap(near, "c")


def columns(axis, *values):
    blocks = []
    for step in range(4):
        target = (lax.axis_index(axis) + step) & 3
        share = [
            lax.dynamic_slice_in_dim(v, target * (v.shape[1] // 4), v.shape[1] // 4, 1)
            for v in values
        ]
        share = share[0] if len(share) == 1 else jnp.concatenate(share, axis=1)
        blocks.append(send(share, axis, step) if step else share)
    return blocks


def call(kernel, name, outs, place, *values, scratch=(), flops=0):
    vmem = pl.BlockSpec(memory_space=pltpu.VMEM)
    made = pl.pallas_call(
        kernel,
        in_specs=[pl.BlockSpec(memory_space=pltpu.SMEM)] + [vmem] * len(values),
        out_specs=[vmem] * len(outs),
        out_shape=[jax.ShapeDtypeStruct(shape, kind) for shape, kind in outs],
        scratch_shapes=[pltpu.VMEM(shape, kind) for shape, kind in scratch],
        compiler_params=pltpu.CompilerParams(vmem_limit_bytes=LIMIT),
        cost_estimate=pl.CostEstimate(flops=flops, bytes_accessed=0, transcendentals=0),
        name=name,
    )(place, *values)
    return made[0] if len(outs) == 1 else list(made)


def flip_kernel(place_ref, in_ref, out_ref):
    out_ref[...] = jnp.transpose(in_ref[...])


def flip(place, values):
    return call(flip_kernel, "flip", [(values.shape[::-1], jnp.bfloat16)], place, values)


def weight_loop(order, sets, put):
    count = len(order)
    for _, _, blocks, gathered in sets:
        for i, block in enumerate(blocks or ()):
            gathered[i * HALF : (i + 1) * HALF] = block[:HALF]
            gathered[(i + count) * HALF : (i + count + 1) * HALF] = block[HALF:]

    @pl.loop(0, 2048 // STEP)
    def _(t):
        at = pl.ds(pl.multiple_of(t * STEP, STEP), STEP)
        totals = []
        for near_ref, far_ref, _, gathered in sets:
            rows = jnp.concatenate(
                [near_ref[i, at] for i in order] + [far_ref[i, at] for i in order], axis=1
            )
            totals.append(product(rows, gathered[...]).astype(jnp.bfloat16))
        total = totals[0] if len(totals) == 1 else jnp.concatenate(totals, axis=1)
        put(t, total.reshape(8, STEP // 8, total.shape[1]))


def shifts(place_ref, along):
    return [(place_ref[along] - step) & 3 for step in range(4)]


def weight_sets(refs, count):
    scratch = refs[len(refs) - count :]
    sets = [
        (refs[6 * n], refs[6 * n + 1], refs[6 * n + 2 : 6 * n + 6], scratch[n])
        for n in range(count)
    ]
    return sets, refs[6 * count : len(refs) - count]


def weight_call(kernel, name, outs, place, *sets):
    values = [value for (near, far), blocks in sets for value in (near, far, *blocks)]
    widths = [blocks[0].shape[1] for _, blocks in sets]
    rows = 64
    return call(
        kernel,
        name,
        [(shape + (rows, sum(widths)), jnp.bfloat16) for shape in outs],
        place,
        *values,
        scratch=[((4 * ROWS, width), jnp.bfloat16) for width in widths],
        flops=7 * 10**9,
    )


def weight_kernel(along, place_ref, *refs):
    sets, (out,) = weight_sets(refs, 1)

    def put(t, total):
        for i in range(8):
            out[t, i // 4, i % 4] = total[i]

    weight_loop(shifts(place_ref, along), sets, put)


def weight_parts(place, along, shared, blocks):
    return weight_call(
        functools.partial(weight_kernel, along),
        "weight_parts",
        [(4, 2, 4)],
        place,
        (shared, blocks),
    )


def weight_sides_kernel(place_ref, *refs):
    sets, (out,) = weight_sets(refs, 1)

    def put(t, total):
        for i in range(8):
            out[t, (i // 4) ^ place_ref[1], (i - place_ref[2]) & 3] = total[i]

    weight_loop(shifts(place_ref, 2), sets, put)


def weight_sides(place, shared, blocks):
    return weight_call(weight_sides_kernel, "weight_sides", [(4, 2, 4)], place, (shared, blocks))


def weight_wide_kernel(place_ref, near_ref, far_ref, gate_ref, up_ref, mine, theirs, gathered):
    def put(t, total):
        column = (t - place_ref[0]) & 3
        for i in range(8):
            step = (i - place_ref[2]) & 3

            @pl.when(place_ref[1] == i // 4)
            def _():
                mine[column, step] = total[i]

            @pl.when(place_ref[1] != i // 4)
            def _():
                theirs[column, step] = total[i]

    for i in range(16):
        for half in range(2):
            to = slice((i + 16 * half) * HALF, (i + 16 * half + 1) * HALF)
            rows = slice(half * HALF, (half + 1) * HALF)
            gathered[to, :HD] = gate_ref[i, rows]
            gathered[to, HD:] = up_ref[i, rows]
    weight_loop(list(range(16)), [(near_ref, far_ref, None, gathered)], put)


def weight_wide(place, near, far, gate, up):
    width = 2 * HD
    return call(
        weight_wide_kernel,
        "weight_wide",
        [((4, 4, 64, width), jnp.bfloat16)] * 2,
        place,
        near,
        far,
        gate,
        up,
        scratch=[((16 * ROWS, width), jnp.bfloat16)],
        flops=13 * 10**9,
    )


def send_all(pieces, axis):
    return pieces[:1] + [send(pieces[step], axis, step) for step in range(1, 4)]


def sum_side(pieces, side):
    return add_low(*(piece[side] for piece in pieces))


def add_low(*values):
    total = values[0].astype(jnp.float32)
    for value in values[1:]:
        total = total + value.astype(jnp.float32)
    return total.astype(jnp.bfloat16)


def arrange_kernel(place_ref, p0, p1, p2, p3, out):
    width = p0.shape[1]
    for step, piece in enumerate((p0, p1, p2, p3)):
        at = pl.multiple_of(((place_ref[2] - step) & 3) * width, width)
        out[:, pl.ds(at, width)] = piece[...].astype(jnp.float32)


def arrange(place, *pieces):
    rows, width = pieces[0].shape
    return call(arrange_kernel, "arrange", [((rows, 4 * width), jnp.float32)], place, *pieces)


def spread_out_kernel(place_ref, p0, p1, p2, p3, gate_ref, up_ref):
    for step, piece in enumerate((p0, p1, p2, p3)):
        for i in range(4):
            share = ((place_ref[0] - i) & 3) * 4 + ((place_ref[2] - step) & 3)
            at = pl.ds(pl.multiple_of(share * HD, HD), HD)
            part = piece[i].astype(jnp.float32)
            gate_ref[:, at] = part[:, :HD]
            up_ref[:, at] = part[:, HD:]


def spread_out(place, *pieces):
    outs = [((64, 16 * HD), jnp.float32)] * 2
    return call(spread_out_kernel, "spread_out", outs, place, *pieces)


def finish_kernel(place_ref, late_ref, q_ref, k_ref, v_ref, o_ref, qg_ref, kg_ref):
    rows = q_ref.shape[0]

    def term(i, at):
        return late_ref[i, :rows, at].astype(jnp.float32)

    for i in range(4):
        total = term(8 * i, slice(0, 3 * HD))
        for j in range(1, 8):
            total = total + term(8 * i + j, slice(0, 3 * HD))
        for n, out in enumerate((q_ref, k_ref, v_ref)):
            out[:, head_columns(i)] = total[:, head_columns(n)]
        total = term(i, head_columns(3))
        for j in range(1, 8):
            total = total + term(4 * j + i, head_columns(3))
        o_ref[:, head_columns(i)] = total
    gains = late_ref[0, rows:].astype(jnp.float32)
    for i in range(1, 32):
        gains = gains + late_ref[i, rows:].astype(jnp.float32)
    qg_ref[...] = gains[0:1]
    kg_ref[...] = gains[1:2]


def finish(place, late):
    rows, width = late.shape[1] - GAIN_ROWS, late.shape[2]
    return call(
        finish_kernel,
        "finish",
        [((rows, 4 * HD), jnp.float32)] * 4 + [((1, width), jnp.float32)] * 2,
        place,
        late,
    )


def scale_block(row):
    return jnp.transpose(jnp.broadcast_to(row, (HD, ROWS)))


def row_scales(squares):
    return lax.rsqrt(squares / (16 * HD) + epsilon)


def head_columns(h):
    return slice(h * HD, (h + 1) * HD)


def turn_kernel(
    place_ref, q_ref, k_ref, v_ref, square_ref, qg_ref, kg_ref, cos_ref, sin_ref, qo_ref, kvo_ref
):
    def turned(values):
        return (values * cos_ref[...] + pltpu.roll(values, HD // 2, 1) * sin_ref[...]).astype(
            jnp.bfloat16
        )

    scales = row_scales(square_ref[...])
    query_scale, key_scale = scale_block(scales[0:1]), scale_block(scales[1:2])
    for h in range(HEADS):
        at = head_columns(h)
        qo_ref[(h - place_ref[0]) & 3] = turned(q_ref[:, at] * query_scale * qg_ref[:, at])
        keys = turned(k_ref[:, at] * key_scale * kg_ref[:, at])
        values = v_ref[:, at]
        for i in range(4):
            kvo_ref[h, i, 0] = keys
            kvo_ref[h, i, 1] = values


def turn(place, *values):
    return call(
        turn_kernel,
        "turn",
        [((4, ROWS, HD), jnp.bfloat16), ((4, 4, 2, ROWS, HD), jnp.bfloat16)],
        place,
        *values,
    )


def to_rows(values):
    rows = []
    for _ in range(3):
        high = values.astype(jnp.bfloat16).astype(jnp.float32)
        rows += [high[:, :HD], high[:, HD:]]
        values = values - high
    return rows


def row_block(rows):
    rows = rows + [jnp.zeros((1, HD), jnp.float32)] * (EXTRA - len(rows))
    return jnp.concatenate(rows, axis=0).astype(jnp.bfloat16)


def from_rows(block, at):
    block = block.astype(jnp.float32)
    sides = [
        block[at + i : at + i + 1] + block[at + i + 2 : at + i + 3] + block[at + i + 4 : at + i + 5]
        for i in range(2)
    ]
    return jnp.concatenate(sides, axis=1)


def keep(place_ref):
    zone, core = place_ref[2], place_ref[3]
    key_row = lax.broadcasted_iota(jnp.int32, (TILE, ROWS), 0)
    query_row = lax.broadcasted_iota(jnp.int32, (TILE, ROWS), 1)
    flip_bit = core * HALF
    key_pos = (key_row & ~(ROWS - 1)) | ((key_row & (ROWS - 1)) ^ flip_bit)
    query_pos = zone * ROWS + (query_row ^ flip_bit)
    return key_pos <= query_pos


def turn_tiles(turned_ref, kv_ref, which):
    for i in range(4):
        for j in range(4):
            turned_ref[i, :, j * ROWS : (j + 1) * ROWS] = jnp.transpose(kv_ref[i, j, which])


def attend_kernel(place_ref, q_ref, kv_ref, out_ref, turned_ref, max_ref, total_ref, sum_ref):
    turn_tiles(turned_ref, kv_ref, 1)

    @pl.loop(0, 4)
    def _(shift):
        column = (place_ref[0] - shift) & 3
        max_ref[...] = jnp.full_like(max_ref, negative)
        total_ref[...] = jnp.zeros_like(total_ref)
        sum_ref[...] = jnp.zeros_like(sum_ref)

        def tile(i, sides, masked=False):
            at = slice(sides.start * ROWS, sides.stop * ROWS)
            count = sides.stop - sides.start
            queries = q_ref[pl.ds(2 * shift + sides.start, count)].reshape(count * ROWS, HD)
            keys = kv_ref[i, :, 0].reshape(TILE, HD)
            scores = product_right(keys, queries) * (score_scale * log2e)
            if masked:
                scores = jnp.where(keep(place_ref), scores, negative)
            old_max = max_ref[:, at]
            new_max = jnp.maximum(old_max, jnp.max(scores, axis=0, keepdims=True))
            weights = jnp.exp2(scores - new_max)
            fade = jnp.exp2(old_max - new_max)
            max_ref[:, at] = new_max
            total_ref[:, at] = total_ref[:, at] * fade + jnp.sum(weights, axis=0, keepdims=True)
            sum_ref[:, at] = sum_ref[:, at] * fade + product(
                turned_ref[i], weights.astype(jnp.bfloat16)
            )

        @pl.loop(0, column)
        def _(i):
            tile(i, slice(0, 2))

        tile(column, slice(0, 1), masked=True)

        @pl.when(place_ref[1] == 0)
        def _():
            tile(column, slice(1, 2))

        for k in range(2):
            at = slice(k * ROWS, (k + 1) * ROWS)
            total = total_ref[:, at]
            seen = total > 0.0
            safe = jnp.where(seen, total, 1.0)
            lse = jnp.where(seen, max_ref[:, at] / log2e + jnp.log(safe), negative)
            to = column * 2 + (place_ref[1] ^ k)
            out_ref[to, :ROWS] = jnp.transpose(sum_ref[:, at] / safe).astype(jnp.bfloat16)
            out_ref[to, ROWS:] = row_block(to_rows(lse))


def attend(place, queries, keys_values):
    return call(
        attend_kernel,
        "attend",
        [((8, ROWS + EXTRA, HD), jnp.bfloat16)],
        place,
        queries,
        keys_values,
        scratch=[
            ((4, HD, TILE), jnp.bfloat16),
            ((1, 2 * ROWS), jnp.float32),
            ((1, 2 * ROWS), jnp.float32),
            ((HD, 2 * ROWS), jnp.float32),
        ],
    )


def merge_kernel(place_ref, part_ref, context_ref, low_ref, log_ref):
    for h in range(HEADS):
        at = head_columns(h)
        lse = jnp.concatenate([from_rows(part_ref[h, i, ROWS:], 0) for i in range(2)], axis=0)
        most = jnp.max(lse, axis=0, keepdims=True)
        shares = jnp.exp(lse - most)
        total = jnp.sum(shares, axis=0, keepdims=True)
        shares = shares / total
        context = scale_block(shares[0:1]) * part_ref[h, 0, :ROWS].astype(jnp.float32)
        context += scale_block(shares[1:2]) * part_ref[h, 1, :ROWS].astype(jnp.float32)
        context_ref[:, at] = context
        low_ref[:, at] = context.astype(jnp.bfloat16)
        log_ref[h : h + 1] = most + jnp.log(total)


def merge(place, parts):
    wide = (ROWS, HEADS * HD)
    return call(
        merge_kernel,
        "merge",
        [(wide, jnp.float32), (wide, jnp.bfloat16), ((HEADS, ROWS), jnp.float32)],
        place,
        parts,
    )


def spread_kernel(place_ref, grad_ref, context_ref, log_ref, gain_ref, out_ref):
    for h in range(HEADS):
        at = head_columns(h)
        grad = grad_ref[:, at]
        dots = jnp.transpose(grad.astype(jnp.float32) * context_ref[:, at])
        row_dot = jnp.sum(dots, axis=0, keepdims=True)
        rows = row_block(to_rows(log_ref[h : h + 1]) + to_rows(row_dot))
        for i in range(2):
            out_ref[h, i, :ROWS] = grad
            out_ref[h, i, ROWS : ROWS + EXTRA] = rows
            out_ref[h, i, ROWS + EXTRA :] = gain_ref[...].astype(jnp.bfloat16)


def spread(place, *values):
    shape = (4, 2, ROWS + EXTRA + GAINS, HD)
    return call(spread_kernel, "spread", [(shape, jnp.bfloat16)], place, *values)


def attend_back_kernel(
    place_ref, q_ref, grad_ref, kv_ref, d0, d1, d2, d3, dkv_ref,
    turned_ref, total_ref, query_ref, held_ref, stat_ref,
):
    turn_tiles(turned_ref, kv_ref, 0)
    total_ref[...] = jnp.zeros_like(total_ref)

    @pl.loop(0, 4)
    def _(shift):
        column = (place_ref[0] - shift) & 3
        query_ref[...] = jnp.zeros_like(query_ref)
        for k in range(2):
            to = column * 2 + (place_ref[1] ^ k)
            at = slice(k * ROWS, (k + 1) * ROWS)
            held_ref[at] = grad_ref[to, :ROWS]
            rows = grad_ref[to, ROWS : ROWS + EXTRA]
            stat_ref[0:1, at] = from_rows(rows, 0) * log2e
            stat_ref[1:2, at] = from_rows(rows, 6)

        def tile(i, sides, masked=False):
            at = slice(sides.start * ROWS, sides.stop * ROWS)
            count = sides.stop - sides.start
            queries = q_ref[pl.ds(2 * shift + sides.start, count)].reshape(count * ROWS, HD)
            grads = held_ref[at]
            keys = kv_ref[i, :, 0].reshape(TILE, HD)
            values = kv_ref[i, :, 1].reshape(TILE, HD)
            scores = product_right(keys, queries) * (score_scale * log2e) - stat_ref[0:1, at]
            if masked:
                scores = jnp.where(keep(place_ref), scores, negative)
            weights = jnp.exp2(scores)
            weight_grad = product_right(values, grads)
            score_grad = (weights * (weight_grad - stat_ref[1:2, at])).astype(jnp.bfloat16)
            total_ref[i, 1] += product(weights.astype(jnp.bfloat16), grads)
            total_ref[i, 0] += product(score_grad, queries)
            query_ref[:, at] += product(turned_ref[i], score_grad)

        @pl.loop(0, column)
        def _(i):
            tile(i, slice(0, 2))

        tile(column, slice(0, 1), masked=True)

        @pl.when(place_ref[1] == 0)
        def _():
            tile(column, slice(1, 2))

        total = jnp.transpose(query_ref[...] * score_scale).astype(jnp.bfloat16)
        for step, out in enumerate((d0, d1, d2, d3)):

            @pl.when(shift == step)
            def _():
                out[...] = total

    gains = grad_ref[0, ROWS + EXTRA :].astype(jnp.float32)
    for i in range(1, 8):
        gains = gains + grad_ref[i, ROWS + EXTRA :].astype(jnp.float32)
    gains = gains.astype(jnp.bfloat16)
    for i in range(4):
        for j in range(4):
            rows = slice(j * ROWS, (j + 1) * ROWS)
            dkv_ref[i, j, :ROWS] = (total_ref[i, 0, rows] * score_scale).astype(jnp.bfloat16)
            dkv_ref[i, j, ROWS : 2 * ROWS] = total_ref[i, 1, rows].astype(jnp.bfloat16)
            dkv_ref[i, j, 2 * ROWS :] = gains


def attend_back(place, queries, grads, keys_values):
    return call(
        attend_back_kernel,
        "attend_back",
        [((2 * ROWS, HD), jnp.bfloat16)] * 4 + [((4, 4, 2 * ROWS + GAINS, HD), jnp.bfloat16)],
        place,
        queries,
        grads,
        keys_values,
        scratch=[
            ((4, HD, TILE), jnp.bfloat16),
            ((4, 2, TILE, HD), jnp.float32),
            ((HD, 2 * ROWS), jnp.float32),
            ((2 * ROWS, HD), jnp.bfloat16),
            ((2, 2 * ROWS), jnp.float32),
        ],
    )


def turn_back_kernel(
    place_ref, d0, d1, d2, d3, dkv_ref, q_ref, k_ref, qg_ref, kg_ref, cos_ref, sin_ref,
    qo_ref, ko_ref, vo_ref, inner_ref, gain_ref, held_ref,
):
    def turned(values):
        return values * cos_ref[...] - pltpu.roll(values, HD // 2, 1) * sin_ref[...]

    for step, piece in enumerate((d0, d1, d2, d3)):
        held_ref[(place_ref[0] + step) & 3] = piece[...].astype(jnp.float32)
    query_inner = jnp.zeros((ROWS, HD), jnp.float32)
    key_inner = jnp.zeros((ROWS, HD), jnp.float32)
    for h in range(HEADS):
        at = head_columns(h)
        queries = turned(held_ref[h])
        keys = dkv_ref[h, 0, :ROWS].astype(jnp.float32)
        values = dkv_ref[h, 0, ROWS : 2 * ROWS].astype(jnp.float32)
        for i in range(1, 4):
            keys = keys + dkv_ref[h, i, :ROWS].astype(jnp.float32)
            values = values + dkv_ref[h, i, ROWS : 2 * ROWS].astype(jnp.float32)
        keys = turned(keys)
        qo_ref[:, at] = queries
        ko_ref[:, at] = keys
        vo_ref[:, at] = values.astype(jnp.bfloat16)
        query_inner = query_inner + queries * qg_ref[:, at] * q_ref[:, at]
        key_inner = key_inner + keys * kg_ref[:, at] * k_ref[:, at]
    inner_ref[0:1] = jnp.sum(jnp.transpose(query_inner), axis=0, keepdims=True)
    inner_ref[1:2] = jnp.sum(jnp.transpose(key_inner), axis=0, keepdims=True)
    gains = dkv_ref[0, 0, 2 * ROWS :].astype(jnp.float32)
    for i in range(1, 4):
        gains = gains + dkv_ref[0, i, 2 * ROWS :].astype(jnp.float32)
    gain_ref[...] = gains


def turn_back(place, query_grads, key_value_grad, *values):
    wide = (ROWS, HEADS * HD)
    return call(
        turn_back_kernel,
        "turn_back",
        [
            (wide, jnp.float32),
            (wide, jnp.float32),
            (wide, jnp.bfloat16),
            ((2, ROWS), jnp.float32),
            ((GAINS, HD), jnp.float32),
        ],
        place,
        *query_grads,
        key_value_grad,
        *values,
        scratch=[((4, ROWS, HD), jnp.float32)],
    )


def raw_back_kernel(
    place_ref, dq_ref, dk_ref, dv_ref, q_ref, k_ref, square_ref, inner_ref, qg_ref, kg_ref,
    s0, s1, s2, s3, qo_ref, ko_ref, gain_ref, held_ref,
):
    scales = row_scales(square_ref[...])
    bends = scales * scales * scales * (inner_ref[...] / (16 * HD))
    for i, (grad_ref, raw_ref, norm_ref, out_ref) in enumerate(
        [(dq_ref, q_ref, qg_ref, qo_ref), (dk_ref, k_ref, kg_ref, ko_ref)]
    ):
        scale, bend = scale_block(scales[i : i + 1]), scale_block(bends[i : i + 1])
        for h in range(HEADS):
            at = head_columns(h)
            grad = grad_ref[:, at] * scale
            raw = raw_ref[:, at]
            gain_ref[i : i + 1, at] = jnp.sum(grad * raw, axis=0, keepdims=True)
            low = (grad * norm_ref[:, at] - raw * bend).astype(jnp.bfloat16)
            out_ref[:, at] = low
            held_ref[h, :, i * HD : (i + 1) * HD] = low
    for h in range(HEADS):
        held_ref[h, :, 2 * HD :] = dv_ref[:, head_columns(h)]
    for step, out in enumerate((s0, s1, s2, s3)):
        out[...] = held_ref[(place_ref[0] + step) & 3]


def raw_back(place, *values):
    wide = ((ROWS, HEADS * HD), jnp.bfloat16)
    return call(
        raw_back_kernel,
        "raw_back",
        [((ROWS, 3 * HD), jnp.bfloat16)] * 4 + [wide, wide, ((2, HEADS * HD), jnp.float32)],
        place,
        *values,
        scratch=[((4, ROWS, 3 * HD), jnp.bfloat16)],
    )


def per_device(
    tokens,
    query_weight,
    key_weight,
    value_weight,
    output_weight,
    gate_weight,
    up_weight,
    down_weight,
    query_gain,
    key_gain,
    attention_gain,
    feedforward_gain,
    cotangent,
):
    full_width = tokens.shape[1]
    x, yh, z, yl, core = (lax.axis_index(name) for name in AXES)
    place = jnp.stack([x, yh, z, core]).astype(jnp.int32)

    def own_first(values):
        return jnp.where(core == 0, values, jnp.concatenate([values[HALF:], values[:HALF]], axis=0))

    def own_first_columns(values):
        return jnp.where(
            core == 0, values, jnp.concatenate([values[:, HALF:], values[:, :HALF]], axis=1)
        )

    def sum_rows(values):
        return own_first_columns(lax.psum(own_first_columns(values), TP))

    def own_rows(values):
        return lax.dynamic_slice_in_dim(values, core * HALF, HALF, 0)

    def natural_rows(mine):
        theirs = swap(mine, "c")
        return jnp.where(
            core == 0,
            jnp.concatenate([mine, theirs], axis=0),
            jnp.concatenate([theirs, mine], axis=0),
        )

    positions = (8 * x + 4 * yh + z) * ROWS + (jnp.arange(ROWS, dtype=jnp.int32) ^ (core * HALF))
    half_size = HD // 2
    frequency = 1.0 / rope_base ** (jnp.arange(half_size, dtype=jnp.float32) * 2.0 / HD)
    angles = positions.astype(jnp.float32)[:, None] * frequency[None, :]
    cosine, sine = jnp.cos(angles), jnp.sin(angles)
    cosine_table = jnp.concatenate([cosine, cosine], axis=1)
    sine_table = jnp.concatenate([-sine, sine], axis=1)
    query_row_gain, key_row_gain = query_gain[None], key_gain[None]

    tokens_own = own_rows(tokens)
    tokens_first = own_first(tokens)
    query_raw = product(tokens_first, query_weight)
    key_raw = product(tokens_first, key_weight)
    value_low = product(tokens_first, value_weight).astype(jnp.bfloat16)
    squares = jnp.stack(
        [jnp.sum(query_raw * query_raw, axis=1), jnp.sum(key_raw * key_raw, axis=1)]
    )
    squares, value_low = together(squares, value_low)
    squares = sum_rows(squares)
    query_sent, key_value_sent = turn(
        place,
        query_raw,
        key_raw,
        value_low,
        squares,
        query_row_gain,
        key_row_gain,
        cosine_table,
        sine_table,
    )
    query_theirs = swap(query_sent, "yh")
    keys_values = exchange(key_value_sent.reshape(16, 2, ROWS, HD), ("x", "z"))
    queries = [jnp.stack([query_sent[step], query_theirs[step]]) for step in range(4)]
    queries = jnp.stack(queries[:1] + [send(queries[step], "x", step) for step in range(1, 4)])
    queries = queries.reshape(8, ROWS, HD)
    tokens_turned = flip(place, tokens_own)
    keys_values = keys_values.reshape(4, 4, 2, ROWS, HD)
    part = exchange(attend(place, queries, keys_values), ("x", "yh"))
    context, context_low, log_total = merge(place, part.reshape(4, 2, ROWS + EXTRA, HD))
    context_low, tokens_turned = together(context_low, tokens_turned)
    tokens_all = gather(tokens_turned, "x")
    context_columns = columns("z", context_low)

    attn_sum = half_sum(product(context_low, output_weight))
    attn_sum, *context_columns = together(attn_sum, *context_columns)
    attn_scale = lax.rsqrt(jnp.mean(attn_sum * attn_sum, axis=-1, keepdims=True) + epsilon)
    hidden = tokens_own.astype(jnp.float32) + attn_sum * attn_scale * attention_gain
    hidden_own = hidden.astype(jnp.bfloat16)
    hidden_theirs = swap(hidden_own, "c")
    hidden_low = jnp.concatenate([hidden_own, hidden_theirs], axis=0)
    hidden_turned = flip(place, hidden_own)
    hidden_low, hidden_turned = together(hidden_low, hidden_turned)
    hidden_all = gather(hidden_turned, ("x", "z"))
    gate_act = product(hidden_low, gate_weight)
    up_act = product(hidden_low, up_weight)
    gate_sigmoid = jax.nn.sigmoid(gate_act)
    gate_silu = gate_act * gate_sigmoid
    mixed_low = (gate_silu * up_act).astype(jnp.bfloat16)
    mixed_columns = columns("z", mixed_low)

    ffn_part = product(mixed_low, down_weight)
    ffn_sum = half_sum(ffn_part)
    ffn_sum, mixed_columns[1], mixed_columns[3] = together(
        ffn_sum, mixed_columns[1], mixed_columns[3]
    )
    ffn_scale = lax.rsqrt(jnp.mean(ffn_sum * ffn_sum, axis=-1, keepdims=True) + epsilon)
    layer_output = natural_rows(
        (hidden + ffn_sum * ffn_scale * feedforward_gain).astype(jnp.bfloat16)
    )
    upstream = own_rows(cotangent).astype(jnp.float32)
    ffn_gain_term = jnp.sum(upstream * ffn_sum * ffn_scale, axis=0)
    ffn_grad_own = norm_back(ffn_sum, ffn_scale, feedforward_gain, upstream).astype(jnp.bfloat16)
    ffn_grad_theirs = swap(ffn_grad_own, "c")
    ffn_grad = jnp.concatenate([ffn_grad_own, ffn_grad_theirs], axis=0)
    ffn_grad_turned = flip(place, ffn_grad_own)
    mixed_grad = product_right(ffn_grad, down_weight)
    gate_grad = (
        mixed_grad * up_act * gate_sigmoid * (1.0 + gate_act * (1.0 - gate_sigmoid))
    ).astype(jnp.bfloat16)
    up_grad = (mixed_grad * gate_silu).astype(jnp.bfloat16)
    gate_columns = exchange(pack(place, gate_grad), ("x", "z"))
    up_packed = pack(place, up_grad)
    hidden_part = product_right(gate_grad, gate_weight) + product_right(up_grad, up_weight)
    hidden_part, ffn_grad_turned, mixed_columns[2] = together(
        hidden_part, ffn_grad_turned, mixed_columns[2]
    )
    hidden_sum = half_sum(hidden_part)
    hidden_sum, up_packed, tokens_all = together(hidden_sum, up_packed, tokens_all)
    tokens_all = with_other_core(tokens_all)
    hidden_grad = upstream + hidden_sum
    attn_gain_term = jnp.sum(hidden_grad * attn_sum * attn_scale, axis=0)
    attn_grad_own = norm_back(attn_sum, attn_scale, attention_gain, hidden_grad).astype(
        jnp.bfloat16
    )
    attn_grad_theirs = swap(attn_grad_own, "c")
    attn_grad = jnp.concatenate([attn_grad_own, attn_grad_theirs], axis=0)
    attn_grad_turned = flip(place, attn_grad_own)
    context_grad = product_right(attn_grad, output_weight).astype(jnp.bfloat16)
    row_gains = jnp.concatenate([attn_gain_term, ffn_gain_term]).reshape(GAINS, HD)
    row_gains = row_gains + swap(row_gains, "c")
    grad_sent = spread(place, context_grad, context, log_total, row_gains)
    grad_sent, attn_grad_turned, ffn_grad_turned, hidden_all, gate_columns = together(
        grad_sent, attn_grad_turned, ffn_grad_turned, hidden_all, gate_columns
    )
    ffn_grad_all = gather(ffn_grad_turned, "z")
    attn_grad_all = gather(attn_grad_turned, "z")
    hidden_far = swap(hidden_all, "c")
    grad_sent = grad_sent.reshape(8, ROWS + EXTRA + GAINS, HD)
    grads = exchange(grad_sent, ("x", "yh"))
    grads, up_packed = together(grads, up_packed)
    up_columns = exchange(up_packed, ("x", "z"))
    *query_back, key_value_back = attend_back(place, queries, grads, keys_values)
    key_value_back, query_back, up_columns, hidden_far, ffn_grad_all = together(
        key_value_back, query_back, up_columns, hidden_far, ffn_grad_all
    )
    ffn_grad_all = with_other_core(ffn_grad_all)
    key_value_back = exchange(key_value_back.reshape(16, 2 * ROWS + GAINS, HD), ("x", "z"))
    query_theirs = swap(jnp.stack([piece[ROWS:] for piece in query_back]), "yh")
    gate_up_mine, gate_up_theirs = weight_wide(
        place, hidden_all, hidden_far, gate_columns, up_columns
    )
    query_theirs, gate_up_theirs = together(query_theirs, gate_up_theirs)
    gate_up_theirs = swap(gate_up_theirs, "yh")
    query_back = [add_low(query_back[step][:ROWS], query_theirs[step]) for step in range(4)]
    query_back = query_back[:1] + [send(query_back[step], "x", -step) for step in range(1, 4)]
    down_part = weight_sides(place, ffn_grad_all, mixed_columns)
    down_sum = lax.psum_scatter(
        down_part.reshape(full_width, 512), "x", scatter_dimension=0, tiled=True
    ).reshape(2, 4, full_width // 32, 512)
    key_value_back, query_back, gate_up_theirs, down_part = together(
        key_value_back, query_back, gate_up_theirs, down_part
    )
    key_value_back = key_value_back.reshape(4, 4, 2 * ROWS + GAINS, HD)
    query_normed_grad, key_normed_grad, value_grad, inner, row_gains = turn_back(
        place,
        query_back,
        key_value_back,
        query_raw,
        key_raw,
        query_row_gain,
        key_row_gain,
        cosine_table,
        sine_table,
    )
    inner = sum_rows(inner)
    inner, attn_grad_all = together(inner, attn_grad_all)
    attn_grad_all = with_other_core(attn_grad_all)
    *low_sent, query_raw_grad, key_raw_grad, head_gains = raw_back(
        place,
        query_normed_grad,
        key_normed_grad,
        value_grad,
        query_raw,
        key_raw,
        squares,
        inner,
        query_row_gain,
        key_row_gain,
    )
    low_columns = [low_sent[0]] + [send(low_sent[step], "x", step) for step in range(1, 4)]

    gain_rows = jnp.pad(head_gains, ((0, GAIN_ROWS - 2), (0, 0)))[None].astype(jnp.bfloat16)
    output_part = weight_parts(place, 2, attn_grad_all, context_columns)
    low_columns, output_part = together(low_columns, output_part)
    low_part = weight_parts(place, 0, tokens_all, low_columns)
    low_part, query_raw_grad, key_raw_grad = together(low_part, query_raw_grad, key_raw_grad)
    late_sent = jnp.concatenate(
        [
            jnp.concatenate([low_part, output_part], axis=4).reshape(32, full_width // 32, 512),
            jnp.broadcast_to(gain_rows, (32, GAIN_ROWS, 512)),
        ],
        axis=1,
    )
    row_gains = [row_gains[:16].reshape(full_width), row_gains[16:].reshape(full_width)]
    late_sent, gate_up_theirs, row_gains = together(late_sent, gate_up_theirs, row_gains)
    down_theirs = swap(down_sum[1], "yh")
    gate_up_sum = add_low(gate_up_mine, gate_up_theirs)
    gate_up_sum = send_all([gate_up_sum[step] for step in range(4)], "x")
    late = exchange(late_sent, CTX)
    down_sum = [add_low(down_sum[0, step], down_theirs[step]) for step in range(4)]
    down_sum = send_all(down_sum, "z")
    gate_up_sum = send_all(
        [jnp.stack([piece[step] for piece in gate_up_sum]) for step in range(4)], "z"
    )
    tokens_part = (
        product_right(query_raw_grad, query_weight)
        + product_right(key_raw_grad, key_weight)
        + product_right(value_grad, value_weight)
    )
    tokens_grad = natural_rows(hidden_grad + half_sum(tokens_part))
    gate_weight_grad, up_weight_grad = spread_out(place, *gate_up_sum)
    down_weight_grad = arrange(place, *down_sum)
    late, gate_weight_grad, down_weight_grad = together(late, gate_weight_grad, down_weight_grad)
    (
        query_weight_grad,
        key_weight_grad,
        value_weight_grad,
        output_weight_grad,
        query_gain_grad,
        key_gain_grad,
    ) = finish(place, late)
    return (
        layer_output,
        tokens_grad,
        query_weight_grad,
        key_weight_grad,
        value_weight_grad,
        jnp.transpose(output_weight_grad),
        gate_weight_grad,
        up_weight_grad,
        jnp.transpose(down_weight_grad),
        query_gain_grad.reshape(512),
        key_gain_grad.reshape(512),
        row_gains[0],
        row_gains[1],
    )


def solution(mesh):
    chips = Mesh(mesh.devices.reshape(tuple(AXES.values())), tuple(AXES))
    in_specs = (
        P(CTX, None),
        P(None, TP),
        P(None, TP),
        P(None, TP),
        P(TP, None),
        P(None, TP),
        P(None, TP),
        P(TP, None),
        P(TP),
        P(TP),
        P(),
        P(),
        P(CTX, None),
    )
    out_specs = (
        P(CTX, None),
        P(CTX, None),
        P(CTX, TP),
        P(CTX, TP),
        P(CTX, TP),
        P(TP, CTX),
        P(CTX, TP),
        P(CTX, TP),
        P(TP, CTX),
        P(TP),
        P(TP),
        P(),
        P(),
    )
    return jax.shard_map(
        per_device, mesh=chips, in_specs=in_specs, out_specs=out_specs, check_vma=False
    )
```

```python
import functools
import math

import jax
import jax.numpy as jnp
from jax import lax
from jax.experimental import pallas as pl
from jax.experimental.pallas import tpu as pltpu
from jax.sharding import Mesh
from jax.sharding import PartitionSpec as P

HD = 128
AXES = {"x": 4, "yh": 2, "z": 4, "yl": 2, "c": 2}
CTX = ("x", "yh", "z")
TP = ("yl", "c")
ROWS = 256
HALF = 128
HEADS = 4
EXTRA = 16
LIMIT = 60 * 2**20
GAIN_ROWS = 16
STEP = 512
GAINS = 32
TILE = 1024

epsilon = 1e-06
rope_base = 500000.0
negative = -1e30
score_scale = 1.0 / math.sqrt(HD)
log2e = math.log2(math.e)


def product(left, right):
    return jnp.dot(left, right, preferred_element_type=jnp.float32)


def product_left(left, right):
    return lax.dot_general(
        left, right, (((0,), (0,)), ((), ())), preferred_element_type=jnp.float32
    )


def product_right(left, right):
    return lax.dot_general(
        left, right, (((1,), (1,)), ((), ())), preferred_element_type=jnp.float32
    )


def norm_back(values_in, scale_in, gain_in, grad_in):
    scaled_grad = grad_in * gain_in
    inner = jnp.mean(scaled_grad * values_in, axis=-1, keepdims=True)
    return scale_in * scaled_grad - values_in * scale_in**3 * inner


def exchange(values, axes):
    return lax.all_to_all(values, axes, split_axis=0, concat_axis=0, tiled=True)


def swap(values, axis):
    return lax.ppermute(values, axis, [(0, 1), (1, 0)])


def half_sum(part):
    theirs = swap(part[HALF:].astype(jnp.bfloat16), "c")
    mine = (part[:HALF] + theirs.astype(jnp.float32)).astype(jnp.bfloat16)
    far = swap(mine, "yl")
    return mine.astype(jnp.float32) + far.astype(jnp.float32)


def together(*values):
    return lax.optimization_barrier(values)


def send(values, axis, step):
    return lax.ppermute(values, axis, [(i, (i + step) % 4) for i in range(4)])


def gather(half, axis):
    return lax.all_gather(half, axis, axis=0, tiled=True).reshape(-1, half.shape[0], HALF)


def pack_kernel(place_ref, in_ref, out_ref):
    for i in range(16):
        out_ref[i] = in_ref[:, head_columns(i)]


def pack(place, values):
    return call(pack_kernel, "pack", [((16, ROWS, HD), jnp.bfloat16)], place, values)


def with_other_core(near):
    return near, swap(near, "c")


def columns(axis, *values):
    blocks = []
    for step in range(4):
        target = (lax.axis_index(axis) + step) & 3
        share = [
            lax.dynamic_slice_in_dim(v, target * (v.shape[1] // 4), v.shape[1] // 4, 1)
            for v in values
        ]
        share = share[0] if len(share) == 1 else jnp.concatenate(share, axis=1)
        blocks.append(send(share, axis, step) if step else share)
    return blocks


def call(kernel, name, outs, place, *values, scratch=(), flops=0):
    vmem = pl.BlockSpec(memory_space=pltpu.VMEM)
    made = pl.pallas_call(
        kernel,
        in_specs=[pl.BlockSpec(memory_space=pltpu.SMEM)] + [vmem] * len(values),
        out_specs=[vmem] * len(outs),
        out_shape=[jax.ShapeDtypeStruct(shape, kind) for shape, kind in outs],
        scratch_shapes=[pltpu.VMEM(shape, kind) for shape, kind in scratch],
        compiler_params=pltpu.CompilerParams(vmem_limit_bytes=LIMIT),
        cost_estimate=pl.CostEstimate(flops=flops, bytes_accessed=0, transcendentals=0),
        name=name,
    )(place, *values)
    return made[0] if len(outs) == 1 else list(made)


def flip_kernel(place_ref, in_ref, out_ref):
    out_ref[...] = jnp.transpose(in_ref[...])


def flip(place, values):
    return call(flip_kernel, "flip", [(values.shape[::-1], jnp.bfloat16)], place, values)


def weight_loop(order, sets, put):
    count = len(order)
    for _, _, blocks, gathered in sets:
        for i, block in enumerate(blocks or ()):
            gathered[i * HALF : (i + 1) * HALF] = block[:HALF]
            gathered[(i + count) * HALF : (i + count + 1) * HALF] = block[HALF:]

    @pl.loop(0, 2048 // STEP)
    def _(t):
        at = pl.ds(pl.multiple_of(t * STEP, STEP), STEP)
        totals = []
        for near_ref, far_ref, _, gathered in sets:
            rows = jnp.concatenate(
                [near_ref[i, at] for i in order] + [far_ref[i, at] for i in order], axis=1
            )
            totals.append(product(rows, gathered[...]).astype(jnp.bfloat16))
        total = totals[0] if len(totals) == 1 else jnp.concatenate(totals, axis=1)
        put(t, total.reshape(8, STEP // 8, total.shape[1]))


def shifts(place_ref, along):
    return [(place_ref[along] - step) & 3 for step in range(4)]


def weight_sets(refs, count):
    scratch = refs[len(refs) - count :]
    sets = [
        (refs[6 * n], refs[6 * n + 1], refs[6 * n + 2 : 6 * n + 6], scratch[n])
        for n in range(count)
    ]
    return sets, refs[6 * count : len(refs) - count]


def weight_call(kernel, name, outs, place, *sets):
    values = [value for (near, far), blocks in sets for value in (near, far, *blocks)]
    widths = [blocks[0].shape[1] for _, blocks in sets]
    rows = 64
    return call(
        kernel,
        name,
        [(shape + (rows, sum(widths)), jnp.bfloat16) for shape in outs],
        place,
        *values,
        scratch=[((4 * ROWS, width), jnp.bfloat16) for width in widths],
        flops=7 * 10**9,
    )


def weight_kernel(along, place_ref, *refs):
    sets, (out,) = weight_sets(refs, 1)

    def put(t, total):
        for i in range(8):
            out[t, i // 4, i % 4] = total[i]

    weight_loop(shifts(place_ref, along), sets, put)


def weight_parts(place, along, shared, blocks):
    return weight_call(
        functools.partial(weight_kernel, along),
        "weight_parts",
        [(4, 2, 4)],
        place,
        (shared, blocks),
    )


def late_kernel(place_ref, near_ref, far_ref, b0, b1, b2, b3, other_ref, gain_ref, out, gathered):
    width = gathered.shape[1]

    def put(t, total):
        for i in range(8):
            out[t, i // 4, i % 4, :64, :width] = total[i]
            out[t, i // 4, i % 4, :64, width:] = other_ref[t, i // 4, i % 4]
            out[t, i // 4, i % 4, 64:, :] = gain_ref[...]

    sets = [(near_ref, far_ref, (b0, b1, b2, b3), gathered)]
    weight_loop(shifts(place_ref, 0), sets, put)


def late_parts(place, shared, blocks, other, gains):
    width = blocks[0].shape[1]
    shape = (4, 2, 4, 64 + gains.shape[0], width + other.shape[4])
    return call(
        late_kernel,
        "late_parts",
        [(shape, jnp.bfloat16)],
        place,
        *shared,
        *blocks,
        other,
        gains,
        scratch=[((4 * ROWS, width), jnp.bfloat16)],
        flops=7 * 10**9,
    )


def weight_sides_kernel(place_ref, *refs):
    sets, (out,) = weight_sets(refs, 1)

    def put(t, total):
        for i in range(8):
            out[t, i // 4, i % 4] = total[i]

    weight_loop(shifts(place_ref, 2), sets, put)


def weight_sides(place, shared, blocks):
    return weight_call(weight_sides_kernel, "weight_sides", [(4, 2, 4)], place, (shared, blocks))


def weight_wide_kernel(place_ref, near_ref, far_ref, gate_ref, up_ref, mine, theirs, gathered):
    def put(t, total):
        for i in range(8):

            @pl.when(place_ref[1] == i // 4)
            def _():
                mine[t, i % 4] = total[i]

            @pl.when(place_ref[1] != i // 4)
            def _():
                theirs[t, i % 4] = total[i]

    for i in range(16):
        for half in range(2):
            to = slice((i + 16 * half) * HALF, (i + 16 * half + 1) * HALF)
            rows = slice(half * HALF, (half + 1) * HALF)
            gathered[to, :HD] = gate_ref[i, rows]
            gathered[to, HD:] = up_ref[i, rows]
    weight_loop(list(range(16)), [(near_ref, far_ref, None, gathered)], put)


def weight_wide(place, near, far, gate, up):
    width = 2 * HD
    return call(
        weight_wide_kernel,
        "weight_wide",
        [((4, 4, 64, width), jnp.bfloat16)] * 2,
        place,
        near,
        far,
        gate,
        up,
        scratch=[((16 * ROWS, width), jnp.bfloat16)],
    )


def send_all(pieces, axis):
    return pieces[:1] + [send(pieces[step], axis, step) for step in range(1, 4)]


def sum_side(pieces, side):
    return add_low(*(piece[side] for piece in pieces))


def add_low(*values):
    total = values[0].astype(jnp.float32)
    for value in values[1:]:
        total = total + value.astype(jnp.float32)
    return total.astype(jnp.bfloat16)


def arrange_kernel(place_ref, parts_ref, out):
    width = parts_ref.shape[2]
    for i in range(4):
        total = parts_ref[i].astype(jnp.float32) + parts_ref[4 + i].astype(jnp.float32)
        out[:, i * width : (i + 1) * width] = total


def arrange(place, parts):
    _, rows, width = parts.shape
    return call(arrange_kernel, "arrange", [((rows, 4 * width), jnp.float32)], place, parts)


def spread_out_kernel(place_ref, parts_ref, gate_ref, up_ref):
    for i in range(16):
        part = parts_ref[i].astype(jnp.float32)
        gate_ref[:, head_columns(i)] = part[:, :HD]
        up_ref[:, head_columns(i)] = part[:, HD:]


def spread_out(place, parts):
    outs = [((64, 16 * HD), jnp.float32)] * 2
    return call(spread_out_kernel, "spread_out", outs, place, parts)


def finish_kernel(place_ref, late_ref, q_ref, k_ref, v_ref, o_ref, qg_ref, kg_ref):
    rows = q_ref.shape[0]

    def term(i, at):
        return late_ref[i, :rows, at].astype(jnp.float32)

    for i in range(4):
        total = term(8 * i, slice(0, 3 * HD))
        for j in range(1, 8):
            total = total + term(8 * i + j, slice(0, 3 * HD))
        for n, out in enumerate((q_ref, k_ref, v_ref)):
            out[:, head_columns(i)] = total[:, head_columns(n)]
        total = term(i, head_columns(3))
        for j in range(1, 8):
            total = total + term(4 * j + i, head_columns(3))
        o_ref[:, head_columns(i)] = total
    gains = late_ref[0, rows:].astype(jnp.float32)
    for i in range(1, 32):
        gains = gains + late_ref[i, rows:].astype(jnp.float32)
    qg_ref[...] = gains[0:1]
    kg_ref[...] = gains[1:2]


def finish(place, late):
    rows, width = late.shape[1] - GAIN_ROWS, late.shape[2]
    return call(
        finish_kernel,
        "finish",
        [((rows, 4 * HD), jnp.float32)] * 4 + [((1, width), jnp.float32)] * 2,
        place,
        late,
    )


def scale_block(row):
    return jnp.transpose(jnp.broadcast_to(row, (HD, ROWS)))


def row_scales(squares):
    return lax.rsqrt(squares / (16 * HD) + epsilon)


def head_columns(h):
    return slice(h * HD, (h + 1) * HD)


def turn_kernel(
    place_ref, q_ref, k_ref, v_ref, square_ref, qg_ref, kg_ref, cos_ref, sin_ref, qo_ref, kvo_ref
):
    def turned(values):
        return (values * cos_ref[...] + pltpu.roll(values, HD // 2, 1) * sin_ref[...]).astype(
            jnp.bfloat16
        )

    scales = row_scales(square_ref[...])
    query_scale, key_scale = scale_block(scales[0:1]), scale_block(scales[1:2])
    for h in range(HEADS):
        at = head_columns(h)
        qo_ref[(h - place_ref[0]) & 3] = turned(q_ref[:, at] * query_scale * qg_ref[:, at])
        keys = turned(k_ref[:, at] * key_scale * kg_ref[:, at])
        values = v_ref[:, at]
        for i in range(4):
            kvo_ref[h, i, 0] = keys
            kvo_ref[h, i, 1] = values


def turn(place, *values):
    return call(
        turn_kernel,
        "turn",
        [((4, ROWS, HD), jnp.bfloat16), ((4, 4, 2, ROWS, HD), jnp.bfloat16)],
        place,
        *values,
    )


def to_rows(values):
    rows = []
    for _ in range(3):
        high = values.astype(jnp.bfloat16).astype(jnp.float32)
        rows += [high[:, :HD], high[:, HD:]]
        values = values - high
    return rows


def row_block(rows):
    rows = rows + [jnp.zeros((1, HD), jnp.float32)] * (EXTRA - len(rows))
    return jnp.concatenate(rows, axis=0).astype(jnp.bfloat16)


def from_rows(block, at):
    block = block.astype(jnp.float32)
    sides = [
        block[at + i : at + i + 1] + block[at + i + 2 : at + i + 3] + block[at + i + 4 : at + i + 5]
        for i in range(2)
    ]
    return jnp.concatenate(sides, axis=1)


def keep(place_ref):
    zone, core = place_ref[2], place_ref[3]
    key_row = lax.broadcasted_iota(jnp.int32, (TILE, ROWS), 0)
    query_row = lax.broadcasted_iota(jnp.int32, (TILE, ROWS), 1)
    flip_bit = core * HALF
    key_pos = (key_row & ~(ROWS - 1)) | ((key_row & (ROWS - 1)) ^ flip_bit)
    query_pos = zone * ROWS + (query_row ^ flip_bit)
    return key_pos <= query_pos


def turn_tiles(turned_ref, kv_ref, which):
    for i in range(4):
        for j in range(4):
            turned_ref[i, :, j * ROWS : (j + 1) * ROWS] = jnp.transpose(kv_ref[i, j, which])


def attend_kernel(place_ref, q_ref, kv_ref, out_ref, turned_ref, max_ref, total_ref, sum_ref):
    turn_tiles(turned_ref, kv_ref, 1)

    @pl.loop(0, 4)
    def _(shift):
        column = (place_ref[0] - shift) & 3
        max_ref[...] = jnp.full_like(max_ref, negative)
        total_ref[...] = jnp.zeros_like(total_ref)
        sum_ref[...] = jnp.zeros_like(sum_ref)

        def tile(i, sides, masked=False):
            at = slice(sides.start * ROWS, sides.stop * ROWS)
            count = sides.stop - sides.start
            queries = q_ref[pl.ds(2 * shift + sides.start, count)].reshape(count * ROWS, HD)
            keys = kv_ref[i, :, 0].reshape(TILE, HD)
            scores = product_right(keys, queries) * (score_scale * log2e)
            if masked:
                scores = jnp.where(keep(place_ref), scores, negative)
            old_max = max_ref[:, at]
            new_max = jnp.maximum(old_max, jnp.max(scores, axis=0, keepdims=True))
            weights = jnp.exp2(scores - new_max)
            fade = jnp.exp2(old_max - new_max)
            max_ref[:, at] = new_max
            total_ref[:, at] = total_ref[:, at] * fade + jnp.sum(weights, axis=0, keepdims=True)
            sum_ref[:, at] = sum_ref[:, at] * fade + product(
                turned_ref[i], weights.astype(jnp.bfloat16)
            )

        @pl.loop(0, column)
        def _(i):
            tile(i, slice(0, 2))

        tile(column, slice(0, 1), masked=True)

        @pl.when(place_ref[1] == 0)
        def _():
            tile(column, slice(1, 2))

        for k in range(2):
            at = slice(k * ROWS, (k + 1) * ROWS)
            total = total_ref[:, at]
            seen = total > 0.0
            safe = jnp.where(seen, total, 1.0)
            lse = jnp.where(seen, max_ref[:, at] / log2e + jnp.log(safe), negative)
            to = column * 2 + (place_ref[1] ^ k)
            out_ref[to, :ROWS] = jnp.transpose(sum_ref[:, at] / safe).astype(jnp.bfloat16)
            out_ref[to, ROWS:] = row_block(to_rows(lse))


def attend(place, queries, keys_values):
    return call(
        attend_kernel,
        "attend",
        [((8, ROWS + EXTRA, HD), jnp.bfloat16)],
        place,
        queries,
        keys_values,
        scratch=[
            ((4, HD, TILE), jnp.bfloat16),
            ((1, 2 * ROWS), jnp.float32),
            ((1, 2 * ROWS), jnp.float32),
            ((HD, 2 * ROWS), jnp.float32),
        ],
    )


def merge_kernel(place_ref, part_ref, context_ref, low_ref, log_ref):
    for h in range(HEADS):
        at = head_columns(h)
        lse = jnp.concatenate([from_rows(part_ref[h, i, ROWS:], 0) for i in range(2)], axis=0)
        most = jnp.max(lse, axis=0, keepdims=True)
        shares = jnp.exp(lse - most)
        total = jnp.sum(shares, axis=0, keepdims=True)
        shares = shares / total
        context = scale_block(shares[0:1]) * part_ref[h, 0, :ROWS].astype(jnp.float32)
        context += scale_block(shares[1:2]) * part_ref[h, 1, :ROWS].astype(jnp.float32)
        context_ref[:, at] = context
        low_ref[:, at] = context.astype(jnp.bfloat16)
        log_ref[h : h + 1] = most + jnp.log(total)


def merge(place, parts):
    wide = (ROWS, HEADS * HD)
    return call(
        merge_kernel,
        "merge",
        [(wide, jnp.float32), (wide, jnp.bfloat16), ((HEADS, ROWS), jnp.float32)],
        place,
        parts,
    )


def spread_kernel(place_ref, grad_ref, context_ref, log_ref, gain_ref, out_ref):
    for h in range(HEADS):
        at = head_columns(h)
        grad = grad_ref[:, at]
        dots = jnp.transpose(grad.astype(jnp.float32) * context_ref[:, at])
        row_dot = jnp.sum(dots, axis=0, keepdims=True)
        rows = row_block(to_rows(log_ref[h : h + 1]) + to_rows(row_dot))
        for i in range(2):
            out_ref[h, i, :ROWS] = grad
            out_ref[h, i, ROWS : ROWS + EXTRA] = rows
            out_ref[h, i, ROWS + EXTRA :] = gain_ref[...].astype(jnp.bfloat16)


def spread(place, *values):
    shape = (4, 2, ROWS + EXTRA + GAINS, HD)
    return call(spread_kernel, "spread", [(shape, jnp.bfloat16)], place, *values)


def attend_back_kernel(
    place_ref, q_ref, grad_ref, kv_ref, d0, d1, d2, d3, theirs_ref, dkv_ref,
    turned_ref, total_ref, query_ref, held_ref, stat_ref,
):
    turn_tiles(turned_ref, kv_ref, 0)
    total_ref[...] = jnp.zeros_like(total_ref)

    @pl.loop(0, 4)
    def _(shift):
        column = (place_ref[0] - shift) & 3
        query_ref[...] = jnp.zeros_like(query_ref)
        for k in range(2):
            to = column * 2 + (place_ref[1] ^ k)
            at = slice(k * ROWS, (k + 1) * ROWS)
            held_ref[at] = grad_ref[to, :ROWS]
            rows = grad_ref[to, ROWS : ROWS + EXTRA]
            stat_ref[0:1, at] = from_rows(rows, 0) * log2e
            stat_ref[1:2, at] = from_rows(rows, 6)

        def tile(i, sides, masked=False):
            at = slice(sides.start * ROWS, sides.stop * ROWS)
            count = sides.stop - sides.start
            queries = q_ref[pl.ds(2 * shift + sides.start, count)].reshape(count * ROWS, HD)
            grads = held_ref[at]
            keys = kv_ref[i, :, 0].reshape(TILE, HD)
            values = kv_ref[i, :, 1].reshape(TILE, HD)
            scores = product_right(keys, queries) * (score_scale * log2e) - stat_ref[0:1, at]
            if masked:
                scores = jnp.where(keep(place_ref), scores, negative)
            weights = jnp.exp2(scores)
            weight_grad = product_right(values, grads)
            score_grad = (weights * (weight_grad - stat_ref[1:2, at])).astype(jnp.bfloat16)
            total_ref[i, 1] += product(weights.astype(jnp.bfloat16), grads)
            total_ref[i, 0] += product(score_grad, queries)
            query_ref[:, at] += product(turned_ref[i], score_grad)

        @pl.loop(0, column)
        def _(i):
            tile(i, slice(0, 2))

        tile(column, slice(0, 1), masked=True)

        @pl.when(place_ref[1] == 0)
        def _():
            tile(column, slice(1, 2))

        total = jnp.transpose(query_ref[...] * score_scale).astype(jnp.bfloat16)
        theirs_ref[shift] = total[ROWS:]
        for step, out in enumerate((d0, d1, d2, d3)):

            @pl.when(shift == step)
            def _():
                out[...] = total[:ROWS]

    gains = grad_ref[0, ROWS + EXTRA :].astype(jnp.float32)
    for i in range(1, 8):
        gains = gains + grad_ref[i, ROWS + EXTRA :].astype(jnp.float32)
    gains = gains.astype(jnp.bfloat16)
    for i in range(4):
        for j in range(4):
            rows = slice(j * ROWS, (j + 1) * ROWS)
            dkv_ref[i, j, :ROWS] = (total_ref[i, 0, rows] * score_scale).astype(jnp.bfloat16)
            dkv_ref[i, j, ROWS : 2 * ROWS] = total_ref[i, 1, rows].astype(jnp.bfloat16)
            dkv_ref[i, j, 2 * ROWS :] = gains


def attend_back(place, queries, grads, keys_values):
    return call(
        attend_back_kernel,
        "attend_back",
        [((ROWS, HD), jnp.bfloat16)] * 4
        + [((4, ROWS, HD), jnp.bfloat16), ((4, 4, 2 * ROWS + GAINS, HD), jnp.bfloat16)],
        place,
        queries,
        grads,
        keys_values,
        scratch=[
            ((4, HD, TILE), jnp.bfloat16),
            ((4, 2, TILE, HD), jnp.float32),
            ((HD, 2 * ROWS), jnp.float32),
            ((2 * ROWS, HD), jnp.bfloat16),
            ((2, 2 * ROWS), jnp.float32),
        ],
    )


def turn_back_kernel(
    place_ref, d0, d1, d2, d3, dkv_ref, q_ref, k_ref, qg_ref, kg_ref, cos_ref, sin_ref,
    qo_ref, ko_ref, vo_ref, inner_ref, gain_ref, held_ref,
):
    def turned(values):
        return values * cos_ref[...] - pltpu.roll(values, HD // 2, 1) * sin_ref[...]

    for step, piece in enumerate((d0, d1, d2, d3)):
        held_ref[(place_ref[0] + step) & 3] = piece[...].astype(jnp.float32)
    query_inner = jnp.zeros((ROWS, HD), jnp.float32)
    key_inner = jnp.zeros((ROWS, HD), jnp.float32)
    for h in range(HEADS):
        at = head_columns(h)
        queries = turned(held_ref[h])
        keys = dkv_ref[h, 0, :ROWS].astype(jnp.float32)
        values = dkv_ref[h, 0, ROWS : 2 * ROWS].astype(jnp.float32)
        for i in range(1, 4):
            keys = keys + dkv_ref[h, i, :ROWS].astype(jnp.float32)
            values = values + dkv_ref[h, i, ROWS : 2 * ROWS].astype(jnp.float32)
        keys = turned(keys)
        qo_ref[:, at] = queries
        ko_ref[:, at] = keys
        vo_ref[:, at] = values.astype(jnp.bfloat16)
        query_inner = query_inner + queries * qg_ref[:, at] * q_ref[:, at]
        key_inner = key_inner + keys * kg_ref[:, at] * k_ref[:, at]
    inner_ref[0:1] = jnp.sum(jnp.transpose(query_inner), axis=0, keepdims=True)
    inner_ref[1:2] = jnp.sum(jnp.transpose(key_inner), axis=0, keepdims=True)
    gains = dkv_ref[0, 0, 2 * ROWS :].astype(jnp.float32)
    for i in range(1, 4):
        gains = gains + dkv_ref[0, i, 2 * ROWS :].astype(jnp.float32)
    gain_ref[...] = gains


def turn_back(place, query_grads, key_value_grad, *values):
    wide = (ROWS, HEADS * HD)
    return call(
        turn_back_kernel,
        "turn_back",
        [
            (wide, jnp.float32),
            (wide, jnp.float32),
            (wide, jnp.bfloat16),
            ((2, ROWS), jnp.float32),
            ((GAINS, HD), jnp.float32),
        ],
        place,
        *query_grads,
        key_value_grad,
        *values,
        scratch=[((4, ROWS, HD), jnp.float32)],
    )


def raw_back_kernel(
    place_ref, dq_ref, dk_ref, dv_ref, q_ref, k_ref, square_ref, inner_ref, qg_ref, kg_ref,
    s0, s1, s2, s3, qo_ref, ko_ref, gain_ref, held_ref,
):
    scales = row_scales(square_ref[...])
    bends = scales * scales * scales * (inner_ref[...] / (16 * HD))
    for i, (grad_ref, raw_ref, norm_ref, out_ref) in enumerate(
        [(dq_ref, q_ref, qg_ref, qo_ref), (dk_ref, k_ref, kg_ref, ko_ref)]
    ):
        scale, bend = scale_block(scales[i : i + 1]), scale_block(bends[i : i + 1])
        for h in range(HEADS):
            at = head_columns(h)
            grad = grad_ref[:, at] * scale
            raw = raw_ref[:, at]
            gain_ref[i : i + 1, at] = jnp.sum(grad * raw, axis=0, keepdims=True)
            low = (grad * norm_ref[:, at] - raw * bend).astype(jnp.bfloat16)
            out_ref[:, at] = low
            held_ref[h, :, i * HD : (i + 1) * HD] = low
    for h in range(HEADS):
        held_ref[h, :, 2 * HD :] = dv_ref[:, head_columns(h)]
    for step, out in enumerate((s0, s1, s2, s3)):
        out[...] = held_ref[(place_ref[0] + step) & 3]


def raw_back(place, *values):
    wide = ((ROWS, HEADS * HD), jnp.bfloat16)
    return call(
        raw_back_kernel,
        "raw_back",
        [((ROWS, 3 * HD), jnp.bfloat16)] * 4 + [wide, wide, ((2, HEADS * HD), jnp.float32)],
        place,
        *values,
        scratch=[((4, ROWS, 3 * HD), jnp.bfloat16)],
    )


def per_device(
    tokens,
    query_weight,
    key_weight,
    value_weight,
    output_weight,
    gate_weight,
    up_weight,
    down_weight,
    query_gain,
    key_gain,
    attention_gain,
    feedforward_gain,
    cotangent,
):
    full_width = tokens.shape[1]
    x, yh, z, yl, core = (lax.axis_index(name) for name in AXES)
    place = jnp.stack([x, yh, z, core]).astype(jnp.int32)

    def own_first(values):
        return jnp.where(core == 0, values, jnp.concatenate([values[HALF:], values[:HALF]], axis=0))

    def own_first_columns(values):
        return jnp.where(
            core == 0, values, jnp.concatenate([values[:, HALF:], values[:, :HALF]], axis=1)
        )

    def sum_rows(values):
        return own_first_columns(lax.psum(own_first_columns(values), TP))

    def own_rows(values):
        return lax.dynamic_slice_in_dim(values, core * HALF, HALF, 0)

    def natural_rows(mine):
        theirs = swap(mine, "c")
        return jnp.where(
            core == 0,
            jnp.concatenate([mine, theirs], axis=0),
            jnp.concatenate([theirs, mine], axis=0),
        )

    positions = (8 * x + 4 * yh + z) * ROWS + (jnp.arange(ROWS, dtype=jnp.int32) ^ (core * HALF))
    half_size = HD // 2
    frequency = 1.0 / rope_base ** (jnp.arange(half_size, dtype=jnp.float32) * 2.0 / HD)
    angles = positions.astype(jnp.float32)[:, None] * frequency[None, :]
    cosine, sine = jnp.cos(angles), jnp.sin(angles)
    cosine_table = jnp.concatenate([cosine, cosine], axis=1)
    sine_table = jnp.concatenate([-sine, sine], axis=1)
    query_row_gain, key_row_gain = query_gain[None], key_gain[None]

    tokens_own = own_rows(tokens)
    tokens_first = own_first(tokens)
    query_raw = product(tokens_first, query_weight)
    key_raw = product(tokens_first, key_weight)
    value_low = product(tokens_first, value_weight).astype(jnp.bfloat16)
    squares = jnp.stack(
        [jnp.sum(query_raw * query_raw, axis=1), jnp.sum(key_raw * key_raw, axis=1)]
    )
    squares, value_low = together(squares, value_low)
    squares = sum_rows(squares)
    query_sent, key_value_sent = turn(
        place,
        query_raw,
        key_raw,
        value_low,
        squares,
        query_row_gain,
        key_row_gain,
        cosine_table,
        sine_table,
    )
    query_theirs = swap(query_sent, "yh")
    keys_values = exchange(key_value_sent.reshape(16, 2, ROWS, HD), ("x", "z"))
    queries = [jnp.stack([query_sent[step], query_theirs[step]]) for step in range(4)]
    queries = jnp.stack(queries[:1] + [send(queries[step], "x", step) for step in range(1, 4)])
    queries = queries.reshape(8, ROWS, HD)
    tokens_turned = flip(place, tokens_own)
    keys_values = keys_values.reshape(4, 4, 2, ROWS, HD)
    part = exchange(attend(place, queries, keys_values), ("x", "yh"))
    context, context_low, log_total = merge(place, part.reshape(4, 2, ROWS + EXTRA, HD))
    context_low, tokens_turned = together(context_low, tokens_turned)
    tokens_all = gather(tokens_turned, "x")
    context_columns = columns("z", context_low)

    attn_sum = half_sum(product(context_low, output_weight))
    attn_sum, *context_columns = together(attn_sum, *context_columns)
    attn_scale = lax.rsqrt(jnp.mean(attn_sum * attn_sum, axis=-1, keepdims=True) + epsilon)
    hidden = tokens_own.astype(jnp.float32) + attn_sum * attn_scale * attention_gain
    hidden_own = hidden.astype(jnp.bfloat16)
    hidden_theirs = swap(hidden_own, "c")
    hidden_turned = flip(place, hidden_own)
    hidden_theirs, hidden_turned = together(hidden_theirs, hidden_turned)
    hidden_low = jnp.concatenate([hidden_own, hidden_theirs], axis=0)
    hidden_all = gather(hidden_turned, ("x", "z"))
    gate_act = product(hidden_low, gate_weight)
    up_act = product(hidden_low, up_weight)
    gate_sigmoid = jax.nn.sigmoid(gate_act)
    gate_silu = gate_act * gate_sigmoid
    mixed_low = (gate_silu * up_act).astype(jnp.bfloat16)
    mixed_columns = columns("z", mixed_low)

    ffn_part = product(mixed_low, down_weight)
    ffn_sum = half_sum(ffn_part)
    ffn_sum, mixed_columns[1], mixed_columns[3] = together(
        ffn_sum, mixed_columns[1], mixed_columns[3]
    )
    ffn_scale = lax.rsqrt(jnp.mean(ffn_sum * ffn_sum, axis=-1, keepdims=True) + epsilon)
    layer_output = natural_rows(
        (hidden + ffn_sum * ffn_scale * feedforward_gain).astype(jnp.bfloat16)
    )
    upstream = own_rows(cotangent).astype(jnp.float32)
    ffn_gain_term = jnp.sum(upstream * ffn_sum * ffn_scale, axis=0)
    ffn_grad_own = norm_back(ffn_sum, ffn_scale, feedforward_gain, upstream).astype(jnp.bfloat16)
    ffn_grad_theirs = swap(ffn_grad_own, "c")
    ffn_grad = jnp.concatenate([ffn_grad_own, ffn_grad_theirs], axis=0)
    ffn_grad_turned = flip(place, ffn_grad_own)
    mixed_grad = product_right(ffn_grad, down_weight)
    gate_grad = (
        mixed_grad * up_act * gate_sigmoid * (1.0 + gate_act * (1.0 - gate_sigmoid))
    ).astype(jnp.bfloat16)
    up_grad = (mixed_grad * gate_silu).astype(jnp.bfloat16)
    gate_columns = exchange(pack(place, gate_grad), ("x", "z"))
    up_packed = pack(place, up_grad)
    hidden_part = product_right(gate_grad, gate_weight) + product_right(up_grad, up_weight)
    hidden_part, ffn_grad_turned, mixed_columns[2] = together(
        hidden_part, ffn_grad_turned, mixed_columns[2]
    )
    hidden_sum = half_sum(hidden_part)
    hidden_sum, up_packed, tokens_all = together(hidden_sum, up_packed, tokens_all)
    tokens_all = with_other_core(tokens_all)
    hidden_grad = upstream + hidden_sum
    attn_gain_term = jnp.sum(hidden_grad * attn_sum * attn_scale, axis=0)
    attn_grad_own = norm_back(attn_sum, attn_scale, attention_gain, hidden_grad).astype(
        jnp.bfloat16
    )
    attn_grad_theirs = swap(attn_grad_own, "c")
    attn_grad = jnp.concatenate([attn_grad_own, attn_grad_theirs], axis=0)
    attn_grad_turned = flip(place, attn_grad_own)
    context_grad = product_right(attn_grad, output_weight).astype(jnp.bfloat16)
    row_gains = jnp.concatenate([attn_gain_term, ffn_gain_term]).reshape(GAINS, HD)
    row_gains = row_gains + swap(row_gains, "c")
    grad_sent = spread(place, context_grad, context, log_total, row_gains)
    grad_sent, ffn_grad_turned, hidden_all, gate_columns = together(
        grad_sent, ffn_grad_turned, hidden_all, gate_columns
    )
    ffn_grad_all = gather(ffn_grad_turned, "z")
    hidden_far = swap(hidden_all, "c")
    grad_sent = grad_sent.reshape(8, ROWS + EXTRA + GAINS, HD)
    grads = exchange(grad_sent, ("x", "yh"))
    grads, up_packed, attn_grad_turned, layer_output = together(
        grads, up_packed, attn_grad_turned, layer_output
    )
    attn_grad_all = gather(attn_grad_turned, "z")
    up_columns = exchange(up_packed, ("x", "z"))
    *query_back, query_theirs, key_value_back = attend_back(place, queries, grads, keys_values)
    key_value_back, query_theirs, up_columns, hidden_far, ffn_grad_all = together(
        key_value_back, query_theirs, up_columns, hidden_far, ffn_grad_all
    )
    ffn_grad_all = with_other_core(ffn_grad_all)
    key_value_back = exchange(key_value_back.reshape(16, 2 * ROWS + GAINS, HD), ("x", "z"))
    query_theirs = swap(query_theirs, "yh")
    down_part = weight_sides(place, ffn_grad_all, mixed_columns)
    query_theirs, down_part, gate_columns = together(query_theirs, down_part, gate_columns)
    query_back = [add_low(query_back[step], query_theirs[step]) for step in range(4)]
    query_back = query_back[:1] + [send(query_back[step], "x", -step) for step in range(1, 4)]
    gate_up_mine, gate_up_theirs = weight_wide(
        place, hidden_all, hidden_far, gate_columns, up_columns
    )
    gate_up_theirs = swap(gate_up_theirs, "yh")
    down_sum = lax.psum_scatter(
        down_part.reshape(full_width, 512), "x", scatter_dimension=0, tiled=True
    ).reshape(8, full_width // 32, 512)
    key_value_back, query_back, gate_up_theirs = together(
        key_value_back, query_back, gate_up_theirs
    )
    key_value_back = key_value_back.reshape(4, 4, 2 * ROWS + GAINS, HD)
    query_normed_grad, key_normed_grad, value_grad, inner, row_gains = turn_back(
        place,
        query_back,
        key_value_back,
        query_raw,
        key_raw,
        query_row_gain,
        key_row_gain,
        cosine_table,
        sine_table,
    )
    inner = sum_rows(inner)
    inner, attn_grad_all = together(inner, attn_grad_all)
    attn_grad_all = with_other_core(attn_grad_all)
    *low_sent, query_raw_grad, key_raw_grad, head_gains = raw_back(
        place,
        query_normed_grad,
        key_normed_grad,
        value_grad,
        query_raw,
        key_raw,
        squares,
        inner,
        query_row_gain,
        key_row_gain,
    )
    low_columns = [low_sent[0]] + [send(low_sent[step], "x", step) for step in range(1, 4)]

    gain_rows = jnp.pad(head_gains, ((0, GAIN_ROWS - 2), (0, 0))).astype(jnp.bfloat16)
    output_part = weight_parts(place, 2, attn_grad_all, context_columns)
    output_part, gate_up_theirs = together(output_part, gate_up_theirs)
    gate_up_sum = exchange(add_low(gate_up_mine, gate_up_theirs).reshape(16, 64, 256), ("x", "z"))
    low_columns, output_part = together(low_columns, output_part)
    late_sent = late_parts(place, tokens_all, low_columns, output_part, gain_rows)
    row_gains = [row_gains[:16].reshape(full_width), row_gains[16:].reshape(full_width)]
    late_sent, gate_up_sum, down_sum, row_gains, query_raw_grad, key_raw_grad = together(
        late_sent, gate_up_sum, down_sum, row_gains, query_raw_grad, key_raw_grad
    )
    down_sum = exchange(down_sum, ("yh", "z"))
    late_sent, down_sum = together(late_sent, down_sum)
    late_sent = late_sent.reshape(32, 64 + GAIN_ROWS, 512)
    tokens_part = (
        product_right(query_raw_grad, query_weight)
        + product_right(key_raw_grad, key_weight)
        + product_right(value_grad, value_weight)
    )
    late = exchange(late_sent, CTX)
    tokens_grad = natural_rows(hidden_grad + half_sum(tokens_part))
    gate_weight_grad, up_weight_grad = spread_out(place, gate_up_sum)
    down_weight_grad = arrange(place, down_sum)
    (
        query_weight_grad,
        key_weight_grad,
        value_weight_grad,
        output_weight_grad,
        query_gain_grad,
        key_gain_grad,
    ) = finish(place, late)
    return (
        layer_output,
        tokens_grad,
        query_weight_grad,
        key_weight_grad,
        value_weight_grad,
        jnp.transpose(output_weight_grad),
        gate_weight_grad,
        up_weight_grad,
        jnp.transpose(down_weight_grad),
        query_gain_grad.reshape(512),
        key_gain_grad.reshape(512),
        row_gains[0],
        row_gains[1],
    )


def solution(mesh):
    chips = Mesh(mesh.devices.reshape(tuple(AXES.values())), tuple(AXES))
    in_specs = (
        P(CTX, None),
        P(None, TP),
        P(None, TP),
        P(None, TP),
        P(TP, None),
        P(None, TP),
        P(None, TP),
        P(TP, None),
        P(TP),
        P(TP),
        P(),
        P(),
        P(CTX, None),
    )
    out_specs = (
        P(CTX, None),
        P(CTX, None),
        P(CTX, TP),
        P(CTX, TP),
        P(CTX, TP),
        P(TP, CTX),
        P(CTX, TP),
        P(CTX, TP),
        P(TP, CTX),
        P(TP),
        P(TP),
        P(),
        P(),
    )
    return jax.shard_map(
        per_device, mesh=chips, in_specs=in_specs, out_specs=out_specs, check_vma=False
    )
```

```python
import functools
import math

import jax
import jax.numpy as jnp
from jax import lax
from jax.experimental import pallas as pl
from jax.experimental.pallas import tpu as pltpu
from jax.sharding import Mesh
from jax.sharding import PartitionSpec as P

HD = 128
AXES = {"x": 4, "yh": 2, "z": 4, "yl": 2, "c": 2}
CTX = ("x", "yh", "z")
TP = ("yl", "c")
ROWS = 256
HALF = 128
HEADS = 4
EXTRA = 16
LIMIT = 60 * 2**20
GAIN_ROWS = 16
STEP = 512
GAINS = 32
TILE = 1024

epsilon = 1e-06
rope_base = 500000.0
negative = -1e30
score_scale = 1.0 / math.sqrt(HD)
log2e = math.log2(math.e)


def product(left, right):
    return jnp.dot(left, right, preferred_element_type=jnp.float32)


def product_right(left, right):
    return lax.dot_general(
        left, right, (((1,), (1,)), ((), ())), preferred_element_type=jnp.float32
    )


def norm_back(values_in, scale_in, gain_in, grad_in):
    scaled_grad = grad_in * gain_in
    inner = jnp.mean(scaled_grad * values_in, axis=-1, keepdims=True)
    return scale_in * scaled_grad - values_in * scale_in**3 * inner


def exchange(values, axes):
    return lax.all_to_all(values, axes, split_axis=0, concat_axis=0, tiled=True)


def swap(values, axis):
    return lax.ppermute(values, axis, [(0, 1), (1, 0)])


def half_sum(part):
    theirs = swap(part[HALF:].astype(jnp.bfloat16), "c")
    mine = (part[:HALF] + theirs.astype(jnp.float32)).astype(jnp.bfloat16)
    far = swap(mine, "yl")
    return mine.astype(jnp.float32) + far.astype(jnp.float32)


def together(*values):
    return lax.optimization_barrier(values)


def send(values, axis, step):
    return lax.ppermute(values, axis, [(i, (i + step) % 4) for i in range(4)])


def gather(half, axis):
    return lax.all_gather(half, axis, axis=0, tiled=True).reshape(-1, half.shape[0], HALF)


def pack_kernel(place_ref, in_ref, out_ref):
    for i in range(16):
        out_ref[i] = in_ref[:, head_columns(i)]


def pack(place, values):
    return call(pack_kernel, "pack", [((16, ROWS, HD), jnp.bfloat16)], place, values)


def with_other_core(near):
    return near, swap(near, "c")


def columns(axis, *values):
    blocks = []
    for step in range(4):
        target = (lax.axis_index(axis) + step) & 3
        share = [
            lax.dynamic_slice_in_dim(v, target * (v.shape[1] // 4), v.shape[1] // 4, 1)
            for v in values
        ]
        share = share[0] if len(share) == 1 else jnp.concatenate(share, axis=1)
        blocks.append(send(share, axis, step) if step else share)
    return blocks


def call(kernel, name, outs, place, *values, scratch=(), flops=0):
    vmem = pl.BlockSpec(memory_space=pltpu.VMEM)
    made = pl.pallas_call(
        kernel,
        in_specs=[pl.BlockSpec(memory_space=pltpu.SMEM)] + [vmem] * len(values),
        out_specs=[vmem] * len(outs),
        out_shape=[jax.ShapeDtypeStruct(shape, kind) for shape, kind in outs],
        scratch_shapes=[pltpu.VMEM(shape, kind) for shape, kind in scratch],
        compiler_params=pltpu.CompilerParams(vmem_limit_bytes=LIMIT),
        cost_estimate=pl.CostEstimate(flops=flops, bytes_accessed=0, transcendentals=0),
        name=name,
    )(place, *values)
    return made[0] if len(outs) == 1 else list(made)


def flip_kernel(place_ref, in_ref, out_ref):
    out_ref[...] = jnp.transpose(in_ref[...])


def flip(place, values):
    return call(flip_kernel, "flip", [(values.shape[::-1], jnp.bfloat16)], place, values)


def weight_loop(order, sets, put):
    count = len(order)
    for _, _, blocks, gathered in sets:
        for i, block in enumerate(blocks or ()):
            gathered[i * HALF : (i + 1) * HALF] = block[:HALF]
            gathered[(i + count) * HALF : (i + count + 1) * HALF] = block[HALF:]

    @pl.loop(0, 2048 // STEP)
    def _(t):
        at = pl.ds(pl.multiple_of(t * STEP, STEP), STEP)
        totals = []
        for near_ref, far_ref, _, gathered in sets:
            rows = jnp.concatenate(
                [near_ref[i, at] for i in order] + [far_ref[i, at] for i in order], axis=1
            )
            totals.append(product(rows, gathered[...]).astype(jnp.bfloat16))
        total = totals[0] if len(totals) == 1 else jnp.concatenate(totals, axis=1)
        put(t, total.reshape(8, STEP // 8, total.shape[1]))


def shifts(place_ref, along):
    return [(place_ref[along] - step) & 3 for step in range(4)]


def weight_sets(refs, count):
    scratch = refs[len(refs) - count :]
    sets = [
        (refs[6 * n], refs[6 * n + 1], refs[6 * n + 2 : 6 * n + 6], scratch[n])
        for n in range(count)
    ]
    return sets, refs[6 * count : len(refs) - count]


def weight_call(kernel, name, outs, place, *sets):
    values = [value for (near, far), blocks in sets for value in (near, far, *blocks)]
    widths = [blocks[0].shape[1] for _, blocks in sets]
    rows = 64
    return call(
        kernel,
        name,
        [(shape + (rows, sum(widths)), jnp.bfloat16) for shape in outs],
        place,
        *values,
        scratch=[((4 * ROWS, width), jnp.bfloat16) for width in widths],
        flops=7 * 10**9,
    )


def weight_kernel(along, place_ref, *refs):
    sets, (out,) = weight_sets(refs, 1)

    def put(t, total):
        for i in range(8):
            out[t, i // 4, i % 4] = total[i]

    weight_loop(shifts(place_ref, along), sets, put)


def weight_parts(place, along, shared, blocks):
    return weight_call(
        functools.partial(weight_kernel, along),
        "weight_parts",
        [(4, 2, 4)],
        place,
        (shared, blocks),
    )


def late_kernel(place_ref, near_ref, far_ref, b0, b1, b2, b3, other_ref, gain_ref, out, gathered):
    width = gathered.shape[1]

    def put(t, total):
        for i in range(8):
            out[t, i // 4, i % 4, :64, :width] = total[i]
            out[t, i // 4, i % 4, :64, width:] = other_ref[t, i // 4, i % 4]
            out[t, i // 4, i % 4, 64:, :] = gain_ref[...]

    sets = [(near_ref, far_ref, (b0, b1, b2, b3), gathered)]
    weight_loop(shifts(place_ref, 0), sets, put)


def late_parts(place, shared, blocks, other, gains):
    width = blocks[0].shape[1]
    shape = (4, 2, 4, 64 + gains.shape[0], width + other.shape[4])
    return call(
        late_kernel,
        "late_parts",
        [(shape, jnp.bfloat16)],
        place,
        *shared,
        *blocks,
        other,
        gains,
        scratch=[((4 * ROWS, width), jnp.bfloat16)],
        flops=7 * 10**9,
    )


def weight_sides_kernel(place_ref, *refs):
    sets, (out,) = weight_sets(refs, 1)

    def put(t, total):
        for i in range(8):
            out[t, i // 4, i % 4] = total[i]

    weight_loop(shifts(place_ref, 2), sets, put)


def weight_sides(place, shared, blocks):
    return weight_call(weight_sides_kernel, "weight_sides", [(4, 2, 4)], place, (shared, blocks))


def weight_wide_kernel(place_ref, near_ref, far_ref, gate_ref, up_ref, mine, theirs, gathered):
    def put(t, total):
        for i in range(8):

            @pl.when(place_ref[1] == i // 4)
            def _():
                mine[t, i % 4] = total[i]

            @pl.when(place_ref[1] != i // 4)
            def _():
                theirs[t, i % 4] = total[i]

    for i in range(16):
        for half in range(2):
            to = slice((i + 16 * half) * HALF, (i + 16 * half + 1) * HALF)
            rows = slice(half * HALF, (half + 1) * HALF)
            gathered[to, :HD] = gate_ref[i, rows]
            gathered[to, HD:] = up_ref[i, rows]
    weight_loop(list(range(16)), [(near_ref, far_ref, None, gathered)], put)


def weight_wide(place, near, far, gate, up):
    width = 2 * HD
    return call(
        weight_wide_kernel,
        "weight_wide",
        [((4, 4, 64, width), jnp.bfloat16)] * 2,
        place,
        near,
        far,
        gate,
        up,
        scratch=[((16 * ROWS, width), jnp.bfloat16)],
    )


def add_low(*values):
    total = values[0].astype(jnp.float32)
    for value in values[1:]:
        total = total + value.astype(jnp.float32)
    return total.astype(jnp.bfloat16)


def arrange_kernel(place_ref, parts_ref, out):
    width = parts_ref.shape[2]
    for i in range(4):
        total = parts_ref[i].astype(jnp.float32) + parts_ref[4 + i].astype(jnp.float32)
        out[:, i * width : (i + 1) * width] = total


def arrange(place, parts):
    _, rows, width = parts.shape
    return call(arrange_kernel, "arrange", [((rows, 4 * width), jnp.float32)], place, parts)


def spread_out_kernel(place_ref, parts_ref, gate_ref, up_ref):
    for i in range(16):
        part = parts_ref[i].astype(jnp.float32)
        gate_ref[:, head_columns(i)] = part[:, :HD]
        up_ref[:, head_columns(i)] = part[:, HD:]


def spread_out(place, parts):
    outs = [((64, 16 * HD), jnp.float32)] * 2
    return call(spread_out_kernel, "spread_out", outs, place, parts)


def finish_kernel(place_ref, late_ref, q_ref, k_ref, v_ref, o_ref, qg_ref, kg_ref):
    rows = q_ref.shape[0]

    def term(i, at):
        return late_ref[i, :rows, at].astype(jnp.float32)

    for i in range(4):
        total = term(8 * i, slice(0, 3 * HD))
        for j in range(1, 8):
            total = total + term(8 * i + j, slice(0, 3 * HD))
        for n, out in enumerate((q_ref, k_ref, v_ref)):
            out[:, head_columns(i)] = total[:, head_columns(n)]
        total = term(i, head_columns(3))
        for j in range(1, 8):
            total = total + term(4 * j + i, head_columns(3))
        o_ref[:, head_columns(i)] = total
    gains = late_ref[0, rows:].astype(jnp.float32)
    for i in range(1, 32):
        gains = gains + late_ref[i, rows:].astype(jnp.float32)
    qg_ref[...] = gains[0:1]
    kg_ref[...] = gains[1:2]


def finish(place, late):
    rows, width = late.shape[1] - GAIN_ROWS, late.shape[2]
    return call(
        finish_kernel,
        "finish",
        [((rows, 4 * HD), jnp.float32)] * 4 + [((1, width), jnp.float32)] * 2,
        place,
        late,
    )


def scale_block(row):
    return jnp.transpose(jnp.broadcast_to(row, (HD, ROWS)))


def row_scales(squares):
    return lax.rsqrt(squares / (16 * HD) + epsilon)


def head_columns(h):
    return slice(h * HD, (h + 1) * HD)


def turn_kernel(
    place_ref, q_ref, k_ref, v_ref, square_ref, qg_ref, kg_ref, cos_ref, sin_ref, qo_ref, kvo_ref
):
    def turned(values):
        return (values * cos_ref[...] + pltpu.roll(values, HD // 2, 1) * sin_ref[...]).astype(
            jnp.bfloat16
        )

    scales = row_scales(square_ref[...])
    query_scale, key_scale = scale_block(scales[0:1]), scale_block(scales[1:2])
    for h in range(HEADS):
        at = head_columns(h)
        qo_ref[(h - place_ref[0]) & 3] = turned(q_ref[:, at] * query_scale * qg_ref[:, at])
        keys = turned(k_ref[:, at] * key_scale * kg_ref[:, at])
        values = v_ref[:, at]
        for i in range(4):
            kvo_ref[h, i, 0] = keys
            kvo_ref[h, i, 1] = values


def turn(place, *values):
    return call(
        turn_kernel,
        "turn",
        [((4, ROWS, HD), jnp.bfloat16), ((4, 4, 2, ROWS, HD), jnp.bfloat16)],
        place,
        *values,
    )


def to_rows(values):
    rows = []
    for _ in range(3):
        high = values.astype(jnp.bfloat16).astype(jnp.float32)
        rows += [high[:, :HD], high[:, HD:]]
        values = values - high
    return rows


def row_block(rows):
    rows = rows + [jnp.zeros((1, HD), jnp.float32)] * (EXTRA - len(rows))
    return jnp.concatenate(rows, axis=0).astype(jnp.bfloat16)


def from_rows(block, at):
    block = block.astype(jnp.float32)
    sides = [
        block[at + i : at + i + 1] + block[at + i + 2 : at + i + 3] + block[at + i + 4 : at + i + 5]
        for i in range(2)
    ]
    return jnp.concatenate(sides, axis=1)


def keep(place_ref):
    zone, core = place_ref[2], place_ref[3]
    key_row = lax.broadcasted_iota(jnp.int32, (TILE, ROWS), 0)
    query_row = lax.broadcasted_iota(jnp.int32, (TILE, ROWS), 1)
    flip_bit = core * HALF
    key_pos = (key_row & ~(ROWS - 1)) | ((key_row & (ROWS - 1)) ^ flip_bit)
    query_pos = zone * ROWS + (query_row ^ flip_bit)
    return key_pos <= query_pos


def turn_tiles(turned_ref, kv_ref, which):
    for i in range(4):
        for j in range(4):
            turned_ref[i, :, j * ROWS : (j + 1) * ROWS] = jnp.transpose(kv_ref[i, j, which])


def attend_kernel(place_ref, q_ref, kv_ref, out_ref, turned_ref, max_ref, total_ref, sum_ref):
    turn_tiles(turned_ref, kv_ref, 1)

    @pl.loop(0, 4)
    def _(shift):
        column = (place_ref[0] - shift) & 3
        max_ref[...] = jnp.full_like(max_ref, negative)
        total_ref[...] = jnp.zeros_like(total_ref)
        sum_ref[...] = jnp.zeros_like(sum_ref)

        def tile(i, sides, masked=False):
            at = slice(sides.start * ROWS, sides.stop * ROWS)
            count = sides.stop - sides.start
            queries = q_ref[pl.ds(2 * shift + sides.start, count)].reshape(count * ROWS, HD)
            keys = kv_ref[i, :, 0].reshape(TILE, HD)
            scores = product_right(keys, queries) * (score_scale * log2e)
            if masked:
                scores = jnp.where(keep(place_ref), scores, negative)
            old_max = max_ref[:, at]
            new_max = jnp.maximum(old_max, jnp.max(scores, axis=0, keepdims=True))
            weights = jnp.exp2(scores - new_max)
            fade = jnp.exp2(old_max - new_max)
            max_ref[:, at] = new_max
            total_ref[:, at] = total_ref[:, at] * fade + jnp.sum(weights, axis=0, keepdims=True)
            sum_ref[:, at] = sum_ref[:, at] * fade + product(
                turned_ref[i], weights.astype(jnp.bfloat16)
            )

        @pl.loop(0, column)
        def _(i):
            tile(i, slice(0, 2))

        tile(column, slice(0, 1), masked=True)

        @pl.when(place_ref[1] == 0)
        def _():
            tile(column, slice(1, 2))

        for k in range(2):
            at = slice(k * ROWS, (k + 1) * ROWS)
            total = total_ref[:, at]
            seen = total > 0.0
            safe = jnp.where(seen, total, 1.0)
            lse = jnp.where(seen, max_ref[:, at] / log2e + jnp.log(safe), negative)
            to = column * 2 + (place_ref[1] ^ k)
            out_ref[to, :ROWS] = jnp.transpose(sum_ref[:, at] / safe).astype(jnp.bfloat16)
            out_ref[to, ROWS:] = row_block(to_rows(lse))


def attend(place, queries, keys_values):
    return call(
        attend_kernel,
        "attend",
        [((8, ROWS + EXTRA, HD), jnp.bfloat16)],
        place,
        queries,
        keys_values,
        scratch=[
            ((4, HD, TILE), jnp.bfloat16),
            ((1, 2 * ROWS), jnp.float32),
            ((1, 2 * ROWS), jnp.float32),
            ((HD, 2 * ROWS), jnp.float32),
        ],
    )


def merge_kernel(place_ref, part_ref, context_ref, low_ref, log_ref):
    for h in range(HEADS):
        at = head_columns(h)
        lse = jnp.concatenate([from_rows(part_ref[h, i, ROWS:], 0) for i in range(2)], axis=0)
        most = jnp.max(lse, axis=0, keepdims=True)
        shares = jnp.exp(lse - most)
        total = jnp.sum(shares, axis=0, keepdims=True)
        shares = shares / total
        context = scale_block(shares[0:1]) * part_ref[h, 0, :ROWS].astype(jnp.float32)
        context += scale_block(shares[1:2]) * part_ref[h, 1, :ROWS].astype(jnp.float32)
        context_ref[:, at] = context
        low_ref[:, at] = context.astype(jnp.bfloat16)
        log_ref[h : h + 1] = most + jnp.log(total)


def merge(place, parts):
    wide = (ROWS, HEADS * HD)
    return call(
        merge_kernel,
        "merge",
        [(wide, jnp.float32), (wide, jnp.bfloat16), ((HEADS, ROWS), jnp.float32)],
        place,
        parts,
    )


def spread_kernel(place_ref, grad_ref, context_ref, log_ref, gain_ref, out_ref):
    for h in range(HEADS):
        at = head_columns(h)
        grad = grad_ref[:, at]
        dots = jnp.transpose(grad.astype(jnp.float32) * context_ref[:, at])
        row_dot = jnp.sum(dots, axis=0, keepdims=True)
        rows = row_block(to_rows(log_ref[h : h + 1]) + to_rows(row_dot))
        for i in range(2):
            out_ref[h, i, :ROWS] = grad
            out_ref[h, i, ROWS : ROWS + EXTRA] = rows
            out_ref[h, i, ROWS + EXTRA :] = gain_ref[...].astype(jnp.bfloat16)


def spread(place, *values):
    shape = (4, 2, ROWS + EXTRA + GAINS, HD)
    return call(spread_kernel, "spread", [(shape, jnp.bfloat16)], place, *values)


def attend_back_kernel(
    place_ref, q_ref, grad_ref, kv_ref, d0, d1, d2, d3, theirs_ref, dkv_ref,
    turned_ref, total_ref, query_ref, held_ref, stat_ref,
):
    turn_tiles(turned_ref, kv_ref, 0)
    total_ref[...] = jnp.zeros_like(total_ref)

    @pl.loop(0, 4)
    def _(shift):
        column = (place_ref[0] - shift) & 3
        query_ref[...] = jnp.zeros_like(query_ref)
        for k in range(2):
            to = column * 2 + (place_ref[1] ^ k)
            at = slice(k * ROWS, (k + 1) * ROWS)
            held_ref[at] = grad_ref[to, :ROWS]
            rows = grad_ref[to, ROWS : ROWS + EXTRA]
            stat_ref[0:1, at] = from_rows(rows, 0) * log2e
            stat_ref[1:2, at] = from_rows(rows, 6)

        def tile(i, sides, masked=False):
            at = slice(sides.start * ROWS, sides.stop * ROWS)
            count = sides.stop - sides.start
            queries = q_ref[pl.ds(2 * shift + sides.start, count)].reshape(count * ROWS, HD)
            grads = held_ref[at]
            keys = kv_ref[i, :, 0].reshape(TILE, HD)
            values = kv_ref[i, :, 1].reshape(TILE, HD)
            scores = product_right(keys, queries) * (score_scale * log2e) - stat_ref[0:1, at]
            if masked:
                scores = jnp.where(keep(place_ref), scores, negative)
            weights = jnp.exp2(scores)
            weight_grad = product_right(values, grads)
            score_grad = (weights * (weight_grad - stat_ref[1:2, at])).astype(jnp.bfloat16)
            total_ref[i, 1] += product(weights.astype(jnp.bfloat16), grads)
            total_ref[i, 0] += product(score_grad, queries)
            query_ref[:, at] += product(turned_ref[i], score_grad)

        @pl.loop(0, column)
        def _(i):
            tile(i, slice(0, 2))

        tile(column, slice(0, 1), masked=True)

        @pl.when(place_ref[1] == 0)
        def _():
            tile(column, slice(1, 2))

        total = jnp.transpose(query_ref[...] * score_scale).astype(jnp.bfloat16)
        theirs_ref[shift] = total[ROWS:]
        for step, out in enumerate((d0, d1, d2, d3)):

            @pl.when(shift == step)
            def _():
                out[...] = total[:ROWS]

    gains = grad_ref[0, ROWS + EXTRA :].astype(jnp.float32)
    for i in range(1, 8):
        gains = gains + grad_ref[i, ROWS + EXTRA :].astype(jnp.float32)
    gains = gains.astype(jnp.bfloat16)
    for i in range(4):
        for j in range(4):
            rows = slice(j * ROWS, (j + 1) * ROWS)
            dkv_ref[i, j, :ROWS] = (total_ref[i, 0, rows] * score_scale).astype(jnp.bfloat16)
            dkv_ref[i, j, ROWS : 2 * ROWS] = total_ref[i, 1, rows].astype(jnp.bfloat16)
            dkv_ref[i, j, 2 * ROWS :] = gains


def attend_back(place, queries, grads, keys_values):
    return call(
        attend_back_kernel,
        "attend_back",
        [((ROWS, HD), jnp.bfloat16)] * 4
        + [((4, ROWS, HD), jnp.bfloat16), ((4, 4, 2 * ROWS + GAINS, HD), jnp.bfloat16)],
        place,
        queries,
        grads,
        keys_values,
        scratch=[
            ((4, HD, TILE), jnp.bfloat16),
            ((4, 2, TILE, HD), jnp.float32),
            ((HD, 2 * ROWS), jnp.float32),
            ((2 * ROWS, HD), jnp.bfloat16),
            ((2, 2 * ROWS), jnp.float32),
        ],
    )


def turn_back_kernel(
    place_ref, d0, d1, d2, d3, dkv_ref, q_ref, k_ref, qg_ref, kg_ref, cos_ref, sin_ref,
    qo_ref, ko_ref, vo_ref, inner_ref, gain_ref, held_ref,
):
    def turned(values):
        return values * cos_ref[...] - pltpu.roll(values, HD // 2, 1) * sin_ref[...]

    for step, piece in enumerate((d0, d1, d2, d3)):
        held_ref[(place_ref[0] + step) & 3] = piece[...].astype(jnp.float32)
    query_inner = jnp.zeros((ROWS, HD), jnp.float32)
    key_inner = jnp.zeros((ROWS, HD), jnp.float32)
    for h in range(HEADS):
        at = head_columns(h)
        queries = turned(held_ref[h])
        keys = dkv_ref[h, 0, :ROWS].astype(jnp.float32)
        values = dkv_ref[h, 0, ROWS : 2 * ROWS].astype(jnp.float32)
        for i in range(1, 4):
            keys = keys + dkv_ref[h, i, :ROWS].astype(jnp.float32)
            values = values + dkv_ref[h, i, ROWS : 2 * ROWS].astype(jnp.float32)
        keys = turned(keys)
        qo_ref[:, at] = queries
        ko_ref[:, at] = keys
        vo_ref[:, at] = values.astype(jnp.bfloat16)
        query_inner = query_inner + queries * qg_ref[:, at] * q_ref[:, at]
        key_inner = key_inner + keys * kg_ref[:, at] * k_ref[:, at]
    inner_ref[0:1] = jnp.sum(jnp.transpose(query_inner), axis=0, keepdims=True)
    inner_ref[1:2] = jnp.sum(jnp.transpose(key_inner), axis=0, keepdims=True)
    gains = dkv_ref[0, 0, 2 * ROWS :].astype(jnp.float32)
    for i in range(1, 4):
        gains = gains + dkv_ref[0, i, 2 * ROWS :].astype(jnp.float32)
    gain_ref[...] = gains


def turn_back(place, query_grads, key_value_grad, *values):
    wide = (ROWS, HEADS * HD)
    return call(
        turn_back_kernel,
        "turn_back",
        [
            (wide, jnp.float32),
            (wide, jnp.float32),
            (wide, jnp.bfloat16),
            ((2, ROWS), jnp.float32),
            ((GAINS, HD), jnp.float32),
        ],
        place,
        *query_grads,
        key_value_grad,
        *values,
        scratch=[((4, ROWS, HD), jnp.float32)],
    )


def raw_back_kernel(
    place_ref, dq_ref, dk_ref, dv_ref, q_ref, k_ref, square_ref, inner_ref, qg_ref, kg_ref,
    s0, s1, s2, s3, qo_ref, ko_ref, gain_ref, held_ref,
):
    scales = row_scales(square_ref[...])
    bends = scales * scales * scales * (inner_ref[...] / (16 * HD))
    for i, (grad_ref, raw_ref, norm_ref, out_ref) in enumerate(
        [(dq_ref, q_ref, qg_ref, qo_ref), (dk_ref, k_ref, kg_ref, ko_ref)]
    ):
        scale, bend = scale_block(scales[i : i + 1]), scale_block(bends[i : i + 1])
        for h in range(HEADS):
            at = head_columns(h)
            grad = grad_ref[:, at] * scale
            raw = raw_ref[:, at]
            gain_ref[i : i + 1, at] = jnp.sum(grad * raw, axis=0, keepdims=True)
            low = (grad * norm_ref[:, at] - raw * bend).astype(jnp.bfloat16)
            out_ref[:, at] = low
            held_ref[h, :, i * HD : (i + 1) * HD] = low
    for h in range(HEADS):
        held_ref[h, :, 2 * HD :] = dv_ref[:, head_columns(h)]
    for step, out in enumerate((s0, s1, s2, s3)):
        out[...] = held_ref[(place_ref[0] + step) & 3]


def raw_back(place, *values):
    wide = ((ROWS, HEADS * HD), jnp.bfloat16)
    return call(
        raw_back_kernel,
        "raw_back",
        [((ROWS, 3 * HD), jnp.bfloat16)] * 4 + [wide, wide, ((2, HEADS * HD), jnp.float32)],
        place,
        *values,
        scratch=[((4, ROWS, 3 * HD), jnp.bfloat16)],
    )


def per_device(
    tokens,
    query_weight,
    key_weight,
    value_weight,
    output_weight,
    gate_weight,
    up_weight,
    down_weight,
    query_gain,
    key_gain,
    attention_gain,
    feedforward_gain,
    cotangent,
):
    full_width = tokens.shape[1]
    x, yh, z, yl, core = (lax.axis_index(name) for name in AXES)
    place = jnp.stack([x, yh, z, core]).astype(jnp.int32)

    def own_first(values):
        return jnp.where(core == 0, values, jnp.concatenate([values[HALF:], values[:HALF]], axis=0))

    def own_first_columns(values):
        return jnp.where(
            core == 0, values, jnp.concatenate([values[:, HALF:], values[:, :HALF]], axis=1)
        )

    def sum_rows(values):
        return own_first_columns(lax.psum(own_first_columns(values), TP))

    def own_rows(values):
        return lax.dynamic_slice_in_dim(values, core * HALF, HALF, 0)

    def natural_rows(mine):
        theirs = swap(mine, "c")
        return jnp.where(
            core == 0,
            jnp.concatenate([mine, theirs], axis=0),
            jnp.concatenate([theirs, mine], axis=0),
        )

    positions = (8 * x + 4 * yh + z) * ROWS + (jnp.arange(ROWS, dtype=jnp.int32) ^ (core * HALF))
    half_size = HD // 2
    frequency = 1.0 / rope_base ** (jnp.arange(half_size, dtype=jnp.float32) * 2.0 / HD)
    angles = positions.astype(jnp.float32)[:, None] * frequency[None, :]
    cosine, sine = jnp.cos(angles), jnp.sin(angles)
    cosine_table = jnp.concatenate([cosine, cosine], axis=1)
    sine_table = jnp.concatenate([-sine, sine], axis=1)
    query_row_gain, key_row_gain = query_gain[None], key_gain[None]

    tokens_own = own_rows(tokens)
    tokens_first = own_first(tokens)
    query_raw = product(tokens_first, query_weight)
    key_raw = product(tokens_first, key_weight)
    value_low = product(tokens_first, value_weight).astype(jnp.bfloat16)
    squares = jnp.stack(
        [jnp.sum(query_raw * query_raw, axis=1), jnp.sum(key_raw * key_raw, axis=1)]
    )
    squares, value_low = together(squares, value_low)
    squares = sum_rows(squares)
    query_sent, key_value_sent = turn(
        place,
        query_raw,
        key_raw,
        value_low,
        squares,
        query_row_gain,
        key_row_gain,
        cosine_table,
        sine_table,
    )
    query_theirs = swap(query_sent, "yh")
    keys_values = exchange(key_value_sent.reshape(16, 2, ROWS, HD), ("x", "z"))
    queries = [jnp.stack([query_sent[step], query_theirs[step]]) for step in range(4)]
    queries = jnp.stack(queries[:1] + [send(queries[step], "x", step) for step in range(1, 4)])
    queries = queries.reshape(8, ROWS, HD)
    tokens_turned = flip(place, tokens_own)
    keys_values = keys_values.reshape(4, 4, 2, ROWS, HD)
    part = exchange(attend(place, queries, keys_values), ("x", "yh"))
    context, context_low, log_total = merge(place, part.reshape(4, 2, ROWS + EXTRA, HD))
    context_low, tokens_turned = together(context_low, tokens_turned)
    tokens_all = gather(tokens_turned, "x")
    context_columns = columns("z", context_low)

    attn_sum = half_sum(product(context_low, output_weight))
    attn_sum, *context_columns = together(attn_sum, *context_columns)
    attn_scale = lax.rsqrt(jnp.mean(attn_sum * attn_sum, axis=-1, keepdims=True) + epsilon)
    hidden = tokens_own.astype(jnp.float32) + attn_sum * attn_scale * attention_gain
    hidden_own = hidden.astype(jnp.bfloat16)
    hidden_theirs = swap(hidden_own, "c")
    hidden_turned = flip(place, hidden_own)
    hidden_theirs, hidden_turned = together(hidden_theirs, hidden_turned)
    hidden_low = jnp.concatenate([hidden_own, hidden_theirs], axis=0)
    hidden_all = gather(hidden_turned, ("x", "z"))
    gate_act = product(hidden_low, gate_weight)
    up_act = product(hidden_low, up_weight)
    gate_sigmoid = jax.nn.sigmoid(gate_act)
    gate_silu = gate_act * gate_sigmoid
    mixed_low = (gate_silu * up_act).astype(jnp.bfloat16)
    mixed_columns = columns("z", mixed_low)

    ffn_part = product(mixed_low, down_weight)
    ffn_sum = half_sum(ffn_part)
    ffn_sum, mixed_columns[1], mixed_columns[3] = together(
        ffn_sum, mixed_columns[1], mixed_columns[3]
    )
    ffn_scale = lax.rsqrt(jnp.mean(ffn_sum * ffn_sum, axis=-1, keepdims=True) + epsilon)
    layer_output = natural_rows(
        (hidden + ffn_sum * ffn_scale * feedforward_gain).astype(jnp.bfloat16)
    )
    upstream = own_rows(cotangent).astype(jnp.float32)
    ffn_gain_term = jnp.sum(upstream * ffn_sum * ffn_scale, axis=0)
    ffn_grad_own = norm_back(ffn_sum, ffn_scale, feedforward_gain, upstream).astype(jnp.bfloat16)
    ffn_grad_theirs = swap(ffn_grad_own, "c")
    ffn_grad = jnp.concatenate([ffn_grad_own, ffn_grad_theirs], axis=0)
    ffn_grad_turned = flip(place, ffn_grad_own)
    mixed_grad = product_right(ffn_grad, down_weight)
    gate_grad = (
        mixed_grad * up_act * gate_sigmoid * (1.0 + gate_act * (1.0 - gate_sigmoid))
    ).astype(jnp.bfloat16)
    up_grad = (mixed_grad * gate_silu).astype(jnp.bfloat16)
    gate_columns = exchange(pack(place, gate_grad), ("x", "z"))
    up_packed = pack(place, up_grad)
    hidden_part = product_right(gate_grad, gate_weight) + product_right(up_grad, up_weight)
    hidden_part, ffn_grad_turned, mixed_columns[2] = together(
        hidden_part, ffn_grad_turned, mixed_columns[2]
    )
    hidden_sum = half_sum(hidden_part)
    hidden_sum, up_packed, tokens_all = together(hidden_sum, up_packed, tokens_all)
    tokens_all = with_other_core(tokens_all)
    hidden_grad = upstream + hidden_sum
    attn_gain_term = jnp.sum(hidden_grad * attn_sum * attn_scale, axis=0)
    attn_grad_own = norm_back(attn_sum, attn_scale, attention_gain, hidden_grad).astype(
        jnp.bfloat16
    )
    attn_grad_theirs = swap(attn_grad_own, "c")
    attn_grad = jnp.concatenate([attn_grad_own, attn_grad_theirs], axis=0)
    attn_grad_turned = flip(place, attn_grad_own)
    context_grad = product_right(attn_grad, output_weight).astype(jnp.bfloat16)
    row_gains = jnp.concatenate([attn_gain_term, ffn_gain_term]).reshape(GAINS, HD)
    row_gains = row_gains + swap(row_gains, "c")
    grad_sent = spread(place, context_grad, context, log_total, row_gains)
    grad_sent, ffn_grad_turned, hidden_all, gate_columns = together(
        grad_sent, ffn_grad_turned, hidden_all, gate_columns
    )
    ffn_grad_all = gather(ffn_grad_turned, "z")
    hidden_far = swap(hidden_all, "c")
    grad_sent = grad_sent.reshape(8, ROWS + EXTRA + GAINS, HD)
    grads = exchange(grad_sent, ("x", "yh"))
    grads, up_packed, attn_grad_turned, layer_output = together(
        grads, up_packed, attn_grad_turned, layer_output
    )
    attn_grad_all = gather(attn_grad_turned, "z")
    up_columns = exchange(up_packed, ("x", "z"))
    *query_back, query_theirs, key_value_back = attend_back(place, queries, grads, keys_values)
    key_value_back, query_theirs, up_columns, hidden_far, ffn_grad_all = together(
        key_value_back, query_theirs, up_columns, hidden_far, ffn_grad_all
    )
    ffn_grad_all = with_other_core(ffn_grad_all)
    key_value_back = exchange(key_value_back.reshape(16, 2 * ROWS + GAINS, HD), ("x", "z"))
    query_theirs = swap(query_theirs, "yh")
    down_part = weight_sides(place, ffn_grad_all, mixed_columns)
    query_theirs, down_part, gate_columns = together(query_theirs, down_part, gate_columns)
    query_back = [add_low(query_back[step], query_theirs[step]) for step in range(4)]
    query_back = query_back[:1] + [send(query_back[step], "x", -step) for step in range(1, 4)]
    gate_up_mine, gate_up_theirs = weight_wide(
        place, hidden_all, hidden_far, gate_columns, up_columns
    )
    gate_up_theirs = swap(gate_up_theirs, "yh")
    down_sum = lax.psum_scatter(
        down_part.reshape(full_width, 512), "x", scatter_dimension=0, tiled=True
    ).reshape(8, full_width // 32, 512)
    key_value_back, query_back, gate_up_theirs = together(
        key_value_back, query_back, gate_up_theirs
    )
    key_value_back = key_value_back.reshape(4, 4, 2 * ROWS + GAINS, HD)
    query_normed_grad, key_normed_grad, value_grad, inner, row_gains = turn_back(
        place,
        query_back,
        key_value_back,
        query_raw,
        key_raw,
        query_row_gain,
        key_row_gain,
        cosine_table,
        sine_table,
    )
    inner = sum_rows(inner)
    inner, attn_grad_all = together(inner, attn_grad_all)
    attn_grad_all = with_other_core(attn_grad_all)
    *low_sent, query_raw_grad, key_raw_grad, head_gains = raw_back(
        place,
        query_normed_grad,
        key_normed_grad,
        value_grad,
        query_raw,
        key_raw,
        squares,
        inner,
        query_row_gain,
        key_row_gain,
    )
    low_columns = [low_sent[0]] + [send(low_sent[step], "x", step) for step in range(1, 4)]

    gain_rows = jnp.pad(head_gains, ((0, GAIN_ROWS - 2), (0, 0))).astype(jnp.bfloat16)
    output_part = weight_parts(place, 2, attn_grad_all, context_columns)
    output_part, gate_up_theirs = together(output_part, gate_up_theirs)
    gate_up_sum = exchange(add_low(gate_up_mine, gate_up_theirs).reshape(16, 64, 256), ("x", "z"))
    low_columns, output_part = together(low_columns, output_part)
    late_sent = late_parts(place, tokens_all, low_columns, output_part, gain_rows)
    row_gains = [row_gains[:16].reshape(full_width), row_gains[16:].reshape(full_width)]
    late_sent, gate_up_sum, down_sum, row_gains, query_raw_grad, key_raw_grad = together(
        late_sent, gate_up_sum, down_sum, row_gains, query_raw_grad, key_raw_grad
    )
    tokens_part = (
        product_right(query_raw_grad, query_weight)
        + product_right(key_raw_grad, key_weight)
        + product_right(value_grad, value_weight)
    )
    tokens_sum = half_sum(tokens_part)
    down_sum = exchange(down_sum, ("yh", "z"))
    late_sent, down_sum, tokens_sum = together(late_sent, down_sum, tokens_sum)
    late_sent = late_sent.reshape(32, 64 + GAIN_ROWS, 512)
    late = exchange(late_sent, CTX)
    tokens_grad = natural_rows(hidden_grad + tokens_sum)
    gate_weight_grad, up_weight_grad = spread_out(place, gate_up_sum)
    down_weight_grad = arrange(place, down_sum)
    (
        query_weight_grad,
        key_weight_grad,
        value_weight_grad,
        output_weight_grad,
        query_gain_grad,
        key_gain_grad,
    ) = finish(place, late)
    return (
        layer_output,
        tokens_grad,
        query_weight_grad,
        key_weight_grad,
        value_weight_grad,
        jnp.transpose(output_weight_grad),
        gate_weight_grad,
        up_weight_grad,
        jnp.transpose(down_weight_grad),
        query_gain_grad.reshape(512),
        key_gain_grad.reshape(512),
        row_gains[0],
        row_gains[1],
    )


def solution(mesh):
    chips = Mesh(mesh.devices.reshape(tuple(AXES.values())), tuple(AXES))
    in_specs = (
        P(CTX, None),
        P(None, TP),
        P(None, TP),
        P(None, TP),
        P(TP, None),
        P(None, TP),
        P(None, TP),
        P(TP, None),
        P(TP),
        P(TP),
        P(),
        P(),
        P(CTX, None),
    )
    out_specs = (
        P(CTX, None),
        P(CTX, None),
        P(CTX, TP),
        P(CTX, TP),
        P(CTX, TP),
        P(TP, CTX),
        P(CTX, TP),
        P(CTX, TP),
        P(TP, CTX),
        P(TP),
        P(TP),
        P(),
        P(),
    )
    return jax.shard_map(
        per_device, mesh=chips, in_specs=in_specs, out_specs=out_specs, check_vma=False
    )
```
